256 devices in a mesh: row: 16 (over y, x), col: 16 (over z, core).
Axes of the slice: x: 4, y: 4, z: 8, core: 2. Of those that a mesh axis runs over, the one named last changes fastest.
Arguments:
- ancestor_inverse: float32 [16384, 16384], P('row', 'col'), may hold values from -18 to 18, as said below
- panel: float32 [16384, 1024], P(('row', 'col')), may hold values from -0.046875 to 0.046875
- diag_inverse: float32 [1024, 1024], replicated, may hold values from -0.1875 to 0.1875
- inverse_pattern: int32 [64, 64], replicated, may hold values from 0 to 1, as said below
- panel_pattern: int32 [64, 4], replicated, may hold values 0 or 1
Outputs:
- sigma_panel: float32 [16384, 1024], P(('row', 'col'))
- sigma_diag: float32 [1024, 1024], replicated
The draws below stay inside these ranges and needn't reach their ends.
Inputs may be any that keep to these rules, and one draw needn't show every extreme that they name: `ancestor_inverse`: symmetric, so entry (i, j) equals entry (j, i). `inverse_pattern`: 1 marks a kept tile; the pattern is symmetric and every diagonal tile is kept. `panel_pattern`: 1 marks a nonzero tile.
All inputs are finite; a program needn't handle non-finite values.
Results may differ from the reference program's by a relative error of at most 0.000075.
Values sent between devices are 32-bit elements; how exact they have to be, the bound alone decides.
No kernel may reach another device: no remote copies, remote signals or barrier semaphores. Data moves between devices by JAX's collectives and lax.ppermute only.
A program may use at most 128 MiB of HBM per device.

```python
import jax
import jax.numpy as jnp
from jax import lax

J = 1024
TILE = 256
S = 16384
N_COL = 16


def draw_ancestor_inverse(key, part):
    key = jax.random.fold_in(key, 5)
    base = jax.random.normal(key, (S, S), jnp.float32)
    paired = (base + base.T) * 0.70710678
    width = S // N_COL
    index_vals = jnp.arange(S, dtype=jnp.int32)
    same = index_vals[:, None] // width == index_vals[None, :] // width
    boosted = paired * jnp.where(same, 3.0, 1.0).astype(jnp.float32)
    return jnp.clip(boosted, -18.0, 18.0).astype(jnp.float32)


def draw_inverse_pattern(key, part):
    key = jax.random.fold_in(key, 11)
    tiles_count = S // TILE
    scores = jax.random.randint(key, (tiles_count, tiles_count), 0, 64)
    tile_rows = jnp.arange(tiles_count, dtype=jnp.int32)[:, None]
    tile_cols = jnp.arange(tiles_count, dtype=jnp.int32)[None, :]
    limits = 8 + 48 * tile_rows // max(tiles_count - 1, 1)
    keeper = (scores < limits) | (tile_rows == tile_cols)
    keeper = keeper | keeper.T
    return keeper.astype(jnp.int32)


def set_ends(result, own_key, low, top_value):
    index_at = [jax.random.randint(jax.random.fold_in(own_key, axis), (), 0, length) for axis, length in enumerate(result.shape)]
    main_axis = result.shape.index(max(result.shape))
    neighbour = index_at[:main_axis] + [(index_at[main_axis] + 1) % result.shape[main_axis]] + index_at[main_axis + 1:]
    return result.at[tuple(index_at)].set(low).at[tuple(neighbour)].set(top_value)


def steps_of(stream_key, dims, split, smallest, top_value):
    def one(dim, blocks):
        heights = jax.random.uniform(jax.random.fold_in(jax.random.fold_in(stream_key, 6), dim), (blocks,), jnp.float32, smallest / len(split), top_value / len(split))
        return jnp.repeat(jnp.exp(heights), dims[dim] // blocks).reshape((-1,) + (1,) * (len(dims) - dim - 1))

    factor_of = one(*split[0])
    for cut in split[1:]:
        factor_of = factor_of * one(*cut)
    return factor_of


def gaussian(own_key, dims, scale, limit, shards=(), held_as=jnp.bfloat16):
    values = jax.random.normal(own_key, dims, jnp.float32) * scale
    if len(shards) > 0:
        values = steps_of(own_key, dims, shards, -0.22, 0.18) * values
    return jnp.clip(values, min=-limit, max=limit).astype(held_as)


def setup_inputs(seed: int = 0) -> dict:
    streams_of = jax.random.split(jax.random.key(seed), 6)
    return {
        "ancestor_inverse": draw_ancestor_inverse(jax.random.fold_in(streams_of[5], 71), 0),
        "panel": gaussian(streams_of[1], (S, J), S ** -0.5, 0.046875, ((0, 256),), jnp.float32),
        "diag_inverse": gaussian(streams_of[2], (J, J), J ** -0.5, 0.1875, (), jnp.float32),
        "inverse_pattern": draw_inverse_pattern(jax.random.fold_in(streams_of[5], 71), 0),
        "panel_pattern": set_ends((jax.random.randint(streams_of[4], (S // TILE, J // TILE), 0, 3) < 2).astype(jnp.int32), jax.random.fold_in(streams_of[4], 1), 0, 1),
    }


HIGH = lax.Precision.HIGHEST


def reference(ancestor_inverse, panel, diag_inverse, inverse_pattern, panel_pattern):
    inv_factor = jnp.tril(diag_inverse) + jnp.eye(J, dtype=jnp.float32)
    panel_mask = jnp.repeat(jnp.repeat(panel_pattern.astype(jnp.float32), TILE, axis=0), TILE, axis=1)
    scaled_panel = jnp.dot(panel * panel_mask, inv_factor, precision=HIGH)
    blocks = ancestor_inverse.reshape(S // TILE, TILE, S)
    tile_flags = inverse_pattern.astype(jnp.float32)

    def one_block(pair):
        rows_block, flag_row = pair
        column_mask = jnp.repeat(flag_row, TILE)
        return -jnp.dot(rows_block * column_mask[None, :], scaled_panel, precision=HIGH)

    sigma_panel = lax.map(one_block, (blocks, tile_flags)).reshape(S, J)
    sigma_diag = jnp.dot(inv_factor.T, inv_factor, precision=HIGH) - jnp.dot(scaled_panel.T, sigma_panel, precision=HIGH)
    return sigma_panel, sigma_diag
```

```python
import jax
import jax.numpy as jnp
from jax import lax
from jax.sharding import PartitionSpec as P

TILE = 256
HIGH = lax.Precision.HIGH


def z_shift(cols_count, step):
    chips = cols_count // 2
    return [(z * 2 + k, ((z + step) % chips) * 2 + k) for z in range(chips) for k in range(2)]


def gather_col(piece, cols_count):
    chips = cols_count // 2
    col_at = lax.axis_index("col")
    z_at = col_at // 2
    held = jnp.zeros((chips,) + piece.shape, piece.dtype)
    held = lax.dynamic_update_slice(held, piece[None], (z_at, 0, 0))
    up = down = piece
    for step in range(1, chips // 2 + 1):
        up = lax.ppermute(up, "col", z_shift(cols_count, 1))
        held = lax.dynamic_update_slice(held, up[None], ((z_at - step) % chips, 0, 0))
        if step < chips // 2:
            down = lax.ppermute(down, "col", z_shift(cols_count, -1))
            held = lax.dynamic_update_slice(held, down[None], ((z_at + step) % chips, 0, 0))
    other = lax.ppermute(held, "col", [(i, i ^ 1) for i in range(cols_count)])
    first = col_at % 2 == 0
    both = jnp.stack([jnp.where(first, held, other), jnp.where(first, other, held)], axis=1)
    return both.reshape((cols_count * piece.shape[0],) + piece.shape[1:])


def shards(ancestor_inverse, panel, diag_inverse, inverse_pattern, panel_pattern):
    rows_count = lax.axis_size("row")
    cols_count = lax.axis_size("col")
    row_at = lax.axis_index("row")
    col_at = lax.axis_index("col")
    block_rows, block_cols = ancestor_inverse.shape
    piece_rows, width = panel.shape
    inv_factor = jnp.tril(diag_inverse) + jnp.eye(width, dtype=jnp.float32)

    with jax.named_scope("local_scaled"):
        first_row = (row_at * cols_count + col_at) * piece_rows
        flags = lax.dynamic_slice(panel_pattern, (first_row // TILE, 0), (1, width // TILE))
        masked = panel * jnp.repeat(flags.astype(jnp.float32), TILE, axis=1)
        scaled = jnp.dot(masked, inv_factor, precision=HIGH)
    with jax.named_scope("gather_scaled"):
        band = gather_col(scaled, cols_count)
    with jax.named_scope("mask_inverse"):
        row_tiles = block_rows // TILE
        col_tiles = block_cols // TILE
        tile_flags = lax.dynamic_slice(
            inverse_pattern, (row_at * row_tiles, col_at * col_tiles), (row_tiles, col_tiles)
        ).astype(jnp.float32)
        masked_inverse = ancestor_inverse * jnp.repeat(jnp.repeat(tile_flags, TILE, axis=0), TILE, axis=1)
    with jax.named_scope("product"):
        partial = -lax.dot_general(band, masked_inverse, (((0,), (0,)), ((), ())), precision=HIGH)
    with jax.named_scope("sum_row"):
        slice_rows = width // rows_count
        partial = partial.reshape(rows_count, slice_rows, block_cols)
        sigma_t = jnp.sum(lax.all_to_all(partial, "row", 0, 0), axis=0)
    with jax.named_scope("transpose_devices"):
        perm = [(r * cols_count + c, c * cols_count + r) for r in range(rows_count) for c in range(cols_count)]
        sigma_t = lax.ppermute(sigma_t, ("row", "col"), perm)
    with jax.named_scope("quad"):
        quad = jnp.dot(sigma_t, band, precision=HIGH)
        factor_rows = lax.dynamic_slice(inv_factor, (row_at * slice_rows, 0), (slice_rows, width))
        factor_tile = lax.dynamic_slice(factor_rows, (0, col_at * slice_rows), (slice_rows, slice_rows))
        base = lax.dot_general(factor_tile, factor_rows, (((0,), (0,)), ((), ())), precision=HIGH)
        term = base - quad
    with jax.named_scope("sum_diag"):
        term = term.reshape(rows_count, slice_rows // rows_count, width)
        own = jnp.sum(lax.all_to_all(term, "row", 0, 0), axis=0)
        rows = lax.all_to_all(jnp.broadcast_to(own[None], term.shape), "row", 0, 0).reshape(slice_rows, width)
        sigma_diag = gather_col(rows, cols_count)
    with jax.named_scope("sigma_out"):
        pieces = sigma_t.reshape(slice_rows, cols_count, piece_rows).transpose(1, 0, 2)
        pieces = lax.all_to_all(pieces, "col", 0, 0)
        sigma_panel = pieces.reshape(width, piece_rows).T
    return sigma_panel, sigma_diag


def solution(mesh):
    return jax.shard_map(
        shards,
        mesh=mesh,
        in_specs=(P("row", "col"), P(("row", "col"), None), P(), P(), P()),
        out_specs=(P(("row", "col"), None), P()),
        check_vma=False,
    )
```

```python
import jax
import jax.numpy as jnp
from jax import lax
from jax.sharding import PartitionSpec as P

TILE = 256
SIDE = 4
BOTH = ("row", "col")
HIGH = lax.Precision.HIGH


def z_shift(cols_count, step):
    chips = cols_count // 2
    return [(z * 2 + k, ((z + step) % chips) * 2 + k) for z in range(chips) for k in range(2)]


def core_swap(value, cols_count):
    return lax.ppermute(value, "col", [(i, i ^ 1) for i in range(cols_count)])


def by_core(first, mine, other, axis):
    low, high = jnp.where(first, mine, other), jnp.where(first, other, mine)
    return jnp.concatenate([low, high], axis=axis)


def z_ring(piece, cols_count):
    chips = cols_count // 2
    z_at = lax.axis_index("col") // 2
    held = jnp.zeros((chips,) + piece.shape, piece.dtype)
    held = lax.dynamic_update_slice(held, piece[None], (z_at, 0, 0))
    up = down = piece
    for step in range(1, chips // 2 + 1):
        up = lax.ppermute(up, "col", z_shift(cols_count, 1))
        held = lax.dynamic_update_slice(held, up[None], ((z_at - step) % chips, 0, 0))
        if step < chips // 2:
            down = lax.ppermute(down, "col", z_shift(cols_count, -1))
            held = lax.dynamic_update_slice(held, down[None], ((z_at + step) % chips, 0, 0))
    return held


def plane_shift(rows_count, cols_count, step, phase):
    perm = []
    for r in range(rows_count):
        for c in range(cols_count):
            y, x = divmod(r, SIDE)
            if (c + phase) % 2 == 0:
                x = (x + step) % SIDE
            else:
                y = (y + step) % SIDE
            perm.append((r * cols_count + c, (y * SIDE + x) * cols_count + c))
    return perm


def plane_scatter(value, at, rows_count, cols_count, phase):
    parts = value.reshape((SIDE, value.shape[0] // SIDE) + value.shape[1:])
    total = lax.dynamic_index_in_dim(parts, at, 0, keepdims=False)
    for step in range(1, SIDE):
        part = lax.dynamic_index_in_dim(parts, (at + step) % SIDE, 0, keepdims=False)
        total = total + lax.ppermute(part, BOTH, plane_shift(rows_count, cols_count, step, phase))
    return total


def plane_sum(value, rows_count, cols_count, phase):
    moved = [
        lax.ppermute(value, BOTH, plane_shift(rows_count, cols_count, step, phase)) for step in range(1, SIDE)
    ]
    return sum(moved, value)


def shards(ancestor_inverse, panel, diag_inverse, inverse_pattern, panel_pattern):
    rows_count = lax.axis_size("row")
    cols_count = lax.axis_size("col")
    chips = cols_count // 2
    row_at = lax.axis_index("row")
    col_at = lax.axis_index("col")
    core_at = col_at % 2
    z_at = col_at // 2
    first = core_at == 0
    y_at, x_at = row_at // SIDE, row_at % SIDE
    phase_at = (jnp.where(first, x_at, y_at), jnp.where(first, y_at, x_at))
    block_rows, block_cols = ancestor_inverse.shape
    piece_rows, width = panel.shape
    half = width // 2
    slice_rows = half // rows_count
    inv_factor = jnp.tril(diag_inverse) + jnp.eye(width, dtype=jnp.float32)

    with jax.named_scope("local_scaled"):
        first_row = (row_at * cols_count + col_at) * piece_rows
        flags = lax.dynamic_slice(panel_pattern, (first_row // TILE, 0), (1, width // TILE))
        masked = panel * jnp.repeat(flags.astype(jnp.float32), TILE, axis=1)
        scaled = jnp.dot(masked, inv_factor, precision=HIGH)
    with jax.named_scope("gather_scaled"):
        left, right = scaled[:, :half], scaled[:, half:]
        mine = jnp.where(first, left, right)
        came = core_swap(jnp.where(first, right, left), cols_count)
        band_own = z_ring(by_core(first, mine, came, 0), cols_count).reshape(block_rows, half)
        band_other = core_swap(band_own, cols_count)
    with jax.named_scope("mask_inverse"):
        row_tiles = block_rows // TILE
        col_tiles = block_cols // TILE
        tile_flags = lax.dynamic_slice(
            inverse_pattern, (row_at * row_tiles, col_at * col_tiles), (row_tiles, col_tiles)
        ).astype(jnp.float32)
        masked_inverse = ancestor_inverse * jnp.repeat(jnp.repeat(tile_flags, TILE, axis=0), TILE, axis=1)

    turn = []
    for r in range(rows_count):
        for c in range(cols_count):
            y, x = divmod(r, SIDE)
            turn.append((r * cols_count + c, c * cols_count + (x * SIDE + y if c % 2 == 0 else r)))

    def sigma_slice(band):
        with jax.named_scope("product"):
            part = -lax.dot_general(band, masked_inverse, (((0,), (0,)), ((), ())), precision=HIGH)
        with jax.named_scope("sum_row"):
            for phase in range(2):
                part = plane_scatter(part, phase_at[phase], rows_count, cols_count, phase)
        with jax.named_scope("turn"):
            return lax.ppermute(part, BOTH, turn)

    slice_own = sigma_slice(band_own)
    slice_other = sigma_slice(band_other)
    sigma_t = by_core(row_at % 2 == 0, slice_own, slice_other, 0)

    with jax.named_scope("quad"):
        quad = by_core(
            first,
            jnp.dot(sigma_t, band_own, precision=HIGH),
            jnp.dot(sigma_t, band_other, precision=HIGH),
            1,
        )
        share = width // rows_count
        factor_rows = lax.dynamic_slice(inv_factor, (row_at * share, 0), (share, width))
        factor_tile = jnp.concatenate(
            [
                lax.dynamic_slice(factor_rows, (0, part * half + col_at * slice_rows), (share, slice_rows))
                for part in range(2)
            ],
            axis=1,
        )
        base = lax.dot_general(factor_tile, factor_rows, (((0,), (0,)), ((), ())), precision=HIGH)
        term = base - quad
    with jax.named_scope("sum_diag"):
        for phase in range(2):
            term = plane_sum(term, rows_count, cols_count, phase)
    with jax.named_scope("gather_diag"):
        held = z_ring(term, cols_count)
        other = core_swap(held, cols_count)
        pieces = by_core(first, held[:, None], other[:, None], 1)
        pieces = pieces.reshape(cols_count, 2, slice_rows, width)
        sigma_diag = pieces.transpose(1, 0, 2, 3).reshape(width, width)
    with jax.named_scope("sigma_out"):
        lanes = 2 * piece_rows
        got = jnp.zeros((chips, 2 * slice_rows, lanes), jnp.float32)
        for step in range(chips):
            block = lax.dynamic_slice(sigma_t, (0, ((z_at + step) % chips) * lanes), (2 * slice_rows, lanes))
            if step:
                block = lax.ppermute(block, "col", z_shift(cols_count, step))
            got = lax.dynamic_update_slice(got, block[None], ((z_at - step) % chips, 0, 0))
        other = core_swap(got, cols_count)
        pieces = by_core(first, got[:, None], other[:, None], 1)
        pieces = lax.dynamic_slice(
            pieces, (0, 0, 0, core_at * piece_rows), (chips, 2, 2 * slice_rows, piece_rows)
        )
        pieces = pieces.reshape(cols_count, 2, slice_rows, piece_rows)
        sigma_panel = pieces.transpose(1, 0, 2, 3).reshape(width, piece_rows).T
    return sigma_panel, sigma_diag


def solution(mesh):
    return jax.shard_map(
        shards,
        mesh=mesh,
        in_specs=(P("row", "col"), P(("row", "col"), None), P(), P(), P()),
        out_specs=(P(("row", "col"), None), P()),
        check_vma=False,
    )
```

```python
import jax
import jax.numpy as jnp
from jax import lax
from jax.experimental import pallas as pl
from jax.experimental.pallas import tpu as pltpu
from jax.sharding import PartitionSpec as P

TILE = 256
SIDE = 4
LANES = 128
VMEM_BYTES = 40 * 1024 * 1024
BOTH = ("row", "col")
HIGH = lax.Precision.HIGH


def z_shift(cols_count, step):
    chips = cols_count // 2
    return [(z * 2 + k, ((z + step) % chips) * 2 + k) for z in range(chips) for k in range(2)]


def core_swap(value, cols_count):
    return lax.ppermute(value, "col", [(i, i ^ 1) for i in range(cols_count)])


def by_core(first, mine, other, axis):
    low, high = jnp.where(first, mine, other), jnp.where(first, other, mine)
    return jnp.concatenate([low, high], axis=axis)


def z_ring(piece, cols_count):
    chips = cols_count // 2
    z_at = lax.axis_index("col") // 2
    held = jnp.zeros((chips,) + piece.shape, piece.dtype)
    held = lax.dynamic_update_slice(held, piece[None], (z_at, 0, 0))
    up = down = piece
    for step in range(1, chips // 2 + 1):
        up = lax.ppermute(up, "col", z_shift(cols_count, 1))
        held = lax.dynamic_update_slice(held, up[None], ((z_at - step) % chips, 0, 0))
        if step < chips // 2:
            down = lax.ppermute(down, "col", z_shift(cols_count, -1))
            held = lax.dynamic_update_slice(held, down[None], ((z_at + step) % chips, 0, 0))
    return held


def plane_shift(rows_count, cols_count, step, phase):
    perm = []
    for r in range(rows_count):
        for c in range(cols_count):
            y, x = divmod(r, SIDE)
            if (c + phase) % 2 == 0:
                x = (x + step) % SIDE
            else:
                y = (y + step) % SIDE
            perm.append((r * cols_count + c, (y * SIDE + x) * cols_count + c))
    return perm


def plane_scatter(value, at, rows_count, cols_count, phase):
    parts = value.reshape((SIDE, value.shape[0] // SIDE) + value.shape[1:])
    total = lax.dynamic_index_in_dim(parts, at, 0, keepdims=False)
    for step in range(1, SIDE):
        part = lax.dynamic_index_in_dim(parts, (at + step) % SIDE, 0, keepdims=False)
        total = total + lax.ppermute(part, BOTH, plane_shift(rows_count, cols_count, step, phase))
    return total


def plane_sum(value, rows_count, cols_count, phase):
    moved = [
        lax.ppermute(value, BOTH, plane_shift(rows_count, cols_count, step, phase)) for step in range(1, SIDE)
    ]
    return sum(moved, value)


def split(value):
    high = value.astype(jnp.bfloat16)
    return high, (value - high.astype(jnp.float32)).astype(jnp.bfloat16)


def product_kernel(flags_ref, band_ref, inverse_ref, out_ref, high_ref, low_ref):
    tile = pl.program_id(0)

    @pl.when(tile == 0)
    def _():
        high, low = split(-band_ref[...].T)
        high_ref[...] = high
        low_ref[...] = low

    rows = inverse_ref.shape[0]
    masked = jnp.concatenate(
        [inverse_ref[i * TILE : (i + 1) * TILE, :] * flags_ref[i, tile] for i in range(rows // TILE)], axis=0
    )
    high, low = split(masked)
    total = jnp.dot(low_ref[...], high, preferred_element_type=jnp.float32)
    total += jnp.dot(high_ref[...], low, preferred_element_type=jnp.float32)
    total += jnp.dot(high_ref[...], high, preferred_element_type=jnp.float32)
    out_ref[...] = total


def product(flags, band, inverse):
    rows, width = band.shape
    cols = inverse.shape[1]
    return pl.pallas_call(
        product_kernel,
        grid=(cols // TILE,),
        in_specs=[
            pl.BlockSpec(memory_space=pltpu.SMEM),
            pl.BlockSpec((rows, width), lambda j: (0, 0)),
            pl.BlockSpec((rows, TILE), lambda j: (0, j)),
        ],
        out_specs=pl.BlockSpec((width, TILE), lambda j: (0, j)),
        out_shape=jax.ShapeDtypeStruct((width, cols), jnp.float32),
        scratch_shapes=[pltpu.VMEM((width, rows), jnp.bfloat16)] * 2,
        compiler_params=pltpu.CompilerParams(vmem_limit_bytes=VMEM_BYTES),
        cost_estimate=pl.CostEstimate(
            flops=6 * rows * width * cols, bytes_accessed=4 * (rows * width + rows * cols + width * cols), transcendentals=0
        ),
    )(flags, band, inverse)


def unfold_kernel(core_ref, own_ref, other_ref, out_ref):
    chips, rows, kept = own_ref.shape
    part = rows // 2
    blocks = out_ref.shape[0] // LANES
    even = core_ref[0] == 0
    for block in range(blocks):
        at, chip = divmod(block, blocks // 2)
        chip = chip * (LANES // rows)
        strips = []
        for z in range(chip, chip + LANES // rows):
            own = own_ref[z, at * part : (at + 1) * part, :]
            other = other_ref[z, at * part : (at + 1) * part, :]
            strips += [jnp.where(even, own, other), jnp.where(even, other, own)]
        whole = jnp.concatenate(strips, axis=0)
        here = slice(block * LANES, (block + 1) * LANES)
        for step in range(kept // LANES):
            value = whole[:, step * LANES : (step + 1) * LANES]
            to = (block + step) % blocks
            there = slice(to * LANES, (to + 1) * LANES)
            out_ref[here, there] = value
            if 0 < step < blocks // 2:
                out_ref[there, here] = value.T


def unfold(core_at, own, other, width):
    whole = pl.BlockSpec(memory_space=pltpu.VMEM)
    return pl.pallas_call(
        unfold_kernel,
        in_specs=[pl.BlockSpec(memory_space=pltpu.SMEM), whole, whole],
        out_specs=whole,
        out_shape=jax.ShapeDtypeStruct((width, width), jnp.float32),
        compiler_params=pltpu.CompilerParams(vmem_limit_bytes=VMEM_BYTES),
        cost_estimate=pl.CostEstimate(flops=0, bytes_accessed=8 * own.size + 4 * width * width, transcendentals=0),
    )(core_at.reshape(1), own, other)


def shards(ancestor_inverse, panel, diag_inverse, inverse_pattern, panel_pattern):
    rows_count = lax.axis_size("row")
    cols_count = lax.axis_size("col")
    chips = cols_count // 2
    row_at = lax.axis_index("row")
    col_at = lax.axis_index("col")
    core_at = col_at % 2
    z_at = col_at // 2
    first = core_at == 0
    y_at, x_at = row_at // SIDE, row_at % SIDE
    phase_at = (jnp.where(first, x_at, y_at), jnp.where(first, y_at, x_at))
    block_rows, block_cols = ancestor_inverse.shape
    piece_rows, width = panel.shape
    half = width // 2
    slice_rows = half // rows_count
    inv_factor = jnp.tril(diag_inverse) + jnp.eye(width, dtype=jnp.float32)

    with jax.named_scope("local_scaled"):
        first_row = (row_at * cols_count + col_at) * piece_rows
        flags = lax.dynamic_slice(panel_pattern, (first_row // TILE, 0), (1, width // TILE))
        masked = panel * jnp.repeat(flags.astype(jnp.float32), TILE, axis=1)
        scaled = jnp.dot(masked, inv_factor, precision=HIGH)
    with jax.named_scope("gather_scaled"):
        left, right = scaled[:, :half], scaled[:, half:]
        mine = jnp.where(first, left, right)
        came = core_swap(jnp.where(first, right, left), cols_count)
        band_own = z_ring(by_core(first, mine, came, 0), cols_count).reshape(block_rows, half)
        band_other = core_swap(band_own, cols_count)
    row_tiles = block_rows // TILE
    col_tiles = block_cols // TILE
    tile_flags = lax.dynamic_slice(
        inverse_pattern, (row_at * row_tiles, col_at * col_tiles), (row_tiles, col_tiles)
    ).astype(jnp.float32)

    turn = []
    for r in range(rows_count):
        for c in range(cols_count):
            y, x = divmod(r, SIDE)
            turn.append((r * cols_count + c, c * cols_count + (x * SIDE + y if c % 2 == 0 else r)))

    def sigma_slice(band):
        with jax.named_scope("product"):
            part = product(tile_flags, band, ancestor_inverse)
        with jax.named_scope("sum_row"):
            for phase in range(2):
                part = plane_scatter(part, phase_at[phase], rows_count, cols_count, phase)
        with jax.named_scope("turn"):
            return lax.ppermute(part, BOTH, turn)

    slice_own = sigma_slice(band_own)
    slice_other = sigma_slice(band_other)
    sigma_t = by_core(row_at % 2 == 0, slice_own, slice_other, 0)

    with jax.named_scope("sigma_out"):
        lanes = 2 * piece_rows
        got = jnp.zeros((chips, 2 * slice_rows, lanes), jnp.float32)
        for step in range(chips):
            block = lax.dynamic_slice(sigma_t, (0, ((z_at + step) % chips) * lanes), (2 * slice_rows, lanes))
            if step:
                block = lax.ppermute(block, "col", z_shift(cols_count, step))
            got = lax.dynamic_update_slice(got, block[None], ((z_at - step) % chips, 0, 0))
        other = core_swap(got, cols_count)
    with jax.named_scope("quad"):
        quad = by_core(
            first,
            jnp.dot(sigma_t, band_own, precision=HIGH),
            jnp.dot(sigma_t, band_other, precision=HIGH),
            1,
        )
        share = width // rows_count
        factor_rows = lax.dynamic_slice(inv_factor, (row_at * share, 0), (share, width))
        factor_tile = jnp.concatenate(
            [
                lax.dynamic_slice(factor_rows, (0, part * half + col_at * slice_rows), (share, slice_rows))
                for part in range(2)
            ],
            axis=1,
        )
        base = lax.dot_general(factor_tile, factor_rows, (((0,), (0,)), ((), ())), precision=HIGH)
        term = base - quad
    with jax.named_scope("keep_half"):
        kept = width // 2 + LANES
        wrapped = jnp.concatenate([term, term[:, : width // 2]], axis=1)
        starts = [(part * half + col_at * slice_rows) // LANES * LANES for part in range(2)]
        term = jnp.concatenate(
            [
                lax.dynamic_slice(wrapped, (part * slice_rows, starts[part]), (slice_rows, kept))
                for part in range(2)
            ],
            axis=0,
        )
    term, got, other = lax.optimization_barrier((term, got, other))
    with jax.named_scope("sum_diag"):
        for phase in range(2):
            term = plane_sum(term, rows_count, cols_count, phase)
    with jax.named_scope("gather_diag"):
        held = z_ring(term, cols_count)
        sigma_diag = unfold(core_at, held, core_swap(held, cols_count), width)
    with jax.named_scope("sigma_join"):
        pieces = by_core(first, got[:, None], other[:, None], 1)
        pieces = lax.dynamic_slice(
            pieces, (0, 0, 0, core_at * piece_rows), (chips, 2, 2 * slice_rows, piece_rows)
        )
        pieces = pieces.reshape(cols_count, 2, slice_rows, piece_rows)
        sigma_panel = pieces.transpose(1, 0, 2, 3).reshape(width, piece_rows).T
    return sigma_panel, sigma_diag


def solution(mesh):
    return jax.shard_map(
        shards,
        mesh=mesh,
        in_specs=(P("row", "col"), P(("row", "col"), None), P(), P(), P()),
        out_specs=(P(("row", "col"), None), P()),
        check_vma=False,
    )
```

```python
import jax
import jax.numpy as jnp
from jax import lax
from jax.experimental import pallas as pl
from jax.experimental.pallas import tpu as pltpu
from jax.sharding import PartitionSpec as P

TILE = 256
SIDE = 4
LANES = 128
VMEM_BYTES = 40 * 1024 * 1024
BOTH = ("row", "col")
HIGH = lax.Precision.HIGH


def z_shift(cols_count, step):
    chips = cols_count // 2
    return [(z * 2 + k, ((z + step) % chips) * 2 + k) for z in range(chips) for k in range(2)]


def core_swap(value, cols_count):
    return lax.ppermute(value, "col", [(i, i ^ 1) for i in range(cols_count)])


def by_core(first, mine, other, axis):
    low, high = jnp.where(first, mine, other), jnp.where(first, other, mine)
    return jnp.concatenate([low, high], axis=axis)


def z_ring(piece, cols_count, beside=None):
    chips = cols_count // 2
    z_at = lax.axis_index("col") // 2
    held = jnp.zeros((chips,) + piece.shape, piece.dtype)
    held = lax.dynamic_update_slice(held, piece[None], (z_at, 0, 0))
    up = down = piece
    for step in range(1, chips // 2 + 1):
        if beside is not None and step == chips // 2 - 1:
            up, down, beside = lax.optimization_barrier((up, down, beside))
        up = lax.ppermute(up, "col", z_shift(cols_count, 1))
        held = lax.dynamic_update_slice(held, up[None], ((z_at - step) % chips, 0, 0))
        if step < chips // 2:
            down = lax.ppermute(down, "col", z_shift(cols_count, -1))
            held = lax.dynamic_update_slice(held, down[None], ((z_at + step) % chips, 0, 0))
    return held, beside


def plane_shift(rows_count, cols_count, step, phase):
    perm = []
    for r in range(rows_count):
        for c in range(cols_count):
            y, x = divmod(r, SIDE)
            if (c + phase) % 2 == 0:
                x = (x + step) % SIDE
            else:
                y = (y + step) % SIDE
            perm.append((r * cols_count + c, (y * SIDE + x) * cols_count + c))
    return perm


def plane_scatter(value, at, rows_count, cols_count, phase):
    parts = value.reshape((SIDE, value.shape[0] // SIDE) + value.shape[1:])
    total = lax.dynamic_index_in_dim(parts, at, 0, keepdims=False)
    for step in range(1, SIDE):
        part = lax.dynamic_index_in_dim(parts, (at + step) % SIDE, 0, keepdims=False)
        total = total + lax.ppermute(part, BOTH, plane_shift(rows_count, cols_count, step, phase))
    return total


def plane_sum(value, rows_count, cols_count):
    for phase in range(2):
        for bit in (1, 2):
            perm = []
            for r in range(rows_count):
                for c in range(cols_count):
                    other = r ^ (bit if (c + phase) % 2 == 0 else bit * SIDE)
                    perm.append((r * cols_count + c, other * cols_count + c))
            value = value + lax.ppermute(value, BOTH, perm)
    return value


def split(value):
    high = value.astype(jnp.bfloat16)
    return high, (value - high.astype(jnp.float32)).astype(jnp.bfloat16)


def product_kernel(at_ref, pattern_ref, band_ref, inverse_ref, out_ref, high_ref, low_ref):
    rows, cols = inverse_ref.shape
    for i in range(rows // TILE):
        here = slice(i * TILE, (i + 1) * TILE)
        high, low = split(-band_ref[here, :].T)
        high_ref[:, here] = high
        low_ref[:, here] = low
    for j in range(cols // TILE):
        there = slice(j * TILE, (j + 1) * TILE)
        masked = []
        for i in range(rows // TILE):
            flag = pattern_ref[at_ref[0] + i, at_ref[1] + j].astype(jnp.float32)
            masked.append(inverse_ref[i * TILE : (i + 1) * TILE, there] * flag)
        high, low = split(jnp.concatenate(masked, axis=0))
        total = jnp.dot(low_ref[...], high, preferred_element_type=jnp.float32)
        total += jnp.dot(high_ref[...], low, preferred_element_type=jnp.float32)
        total += jnp.dot(high_ref[...], high, preferred_element_type=jnp.float32)
        out_ref[:, there] = total


def product(at, pattern, band, inverse):
    rows, width = band.shape
    cols = inverse.shape[1]
    whole = pl.BlockSpec(memory_space=pltpu.VMEM)
    scalars = pl.BlockSpec(memory_space=pltpu.SMEM)
    return pl.pallas_call(
        product_kernel,
        in_specs=[scalars, scalars, whole, whole],
        out_specs=whole,
        out_shape=jax.ShapeDtypeStruct((width, cols), jnp.float32),
        scratch_shapes=[pltpu.VMEM((width, rows), jnp.bfloat16)] * 2,
        compiler_params=pltpu.CompilerParams(vmem_limit_bytes=VMEM_BYTES),
        cost_estimate=pl.CostEstimate(
            flops=6 * rows * width * cols, bytes_accessed=4 * (rows * width + rows * cols + width * cols), transcendentals=0
        ),
    )(at, pattern, band, inverse)


def pack_kernel(own_ref, other_ref, out_ref):
    piece = LANES // 2
    low = lax.broadcasted_iota(jnp.int32, (own_ref.shape[0], LANES), 1) < piece
    for pair in range(out_ref.shape[0] // 2):
        there = slice(pair * LANES, (pair + 1) * LANES)
        own, other = own_ref[:, there], other_ref[:, there]
        out_ref[2 * pair] = jnp.where(low, own, pltpu.roll(other, piece, 1))
        out_ref[2 * pair + 1] = jnp.where(low, pltpu.roll(own, piece, 1), other)


def pack(own, other, count):
    whole = pl.BlockSpec(memory_space=pltpu.VMEM)
    return pl.pallas_call(
        pack_kernel,
        in_specs=[whole, whole],
        out_specs=whole,
        out_shape=jax.ShapeDtypeStruct((count, own.shape[0], LANES), own.dtype),
        cost_estimate=pl.CostEstimate(flops=0, bytes_accessed=16 * own.size, transcendentals=0),
    )(own, other)


def join_kernel(odd_ref, pieces_ref, out_ref):
    even = odd_ref[0] == 0
    rows, width = out_ref.shape
    for x in range(SIDE):
        crossed = jnp.concatenate([pieces_ref[y * SIDE + x] for y in range(SIDE)], axis=0)
        straight = jnp.concatenate([pieces_ref[x * SIDE + y] for y in range(SIDE)], axis=0)
        turned = jnp.where(even, crossed, straight).T
        own, other = turned[:rows], turned[rows:]
        out_ref[:, x * LANES : (x + 1) * LANES] = jnp.where(even, own, other)
        far = width // 2 + x * LANES
        out_ref[:, far : far + LANES] = jnp.where(even, other, own)


def join(odd, pieces, rows, width):
    return pl.pallas_call(
        join_kernel,
        in_specs=[pl.BlockSpec(memory_space=pltpu.SMEM), pl.BlockSpec(memory_space=pltpu.VMEM)],
        out_specs=pl.BlockSpec(memory_space=pltpu.VMEM),
        out_shape=jax.ShapeDtypeStruct((rows, width), pieces.dtype),
        cost_estimate=pl.CostEstimate(flops=0, bytes_accessed=8 * pieces.size, transcendentals=0),
    )(odd.reshape(1), pieces)


def unfold_kernel(core_ref, own_ref, other_ref, out_ref):
    chips, rows, kept = own_ref.shape
    part = rows // 2
    blocks = out_ref.shape[0] // LANES
    even = core_ref[0] == 0
    for block in range(blocks):
        at, chip = divmod(block, blocks // 2)
        chip = chip * (LANES // rows)
        strips = []
        for z in range(chip, chip + LANES // rows):
            own = own_ref[z, at * part : (at + 1) * part, :]
            other = other_ref[z, at * part : (at + 1) * part, :]
            strips += [jnp.where(even, own, other), jnp.where(even, other, own)]
        whole = jnp.concatenate(strips, axis=0)
        here = slice(block * LANES, (block + 1) * LANES)
        for step in range(kept // LANES):
            value = whole[:, step * LANES : (step + 1) * LANES]
            to = (block + step) % blocks
            there = slice(to * LANES, (to + 1) * LANES)
            out_ref[here, there] = value
            if 0 < step < blocks // 2:
                out_ref[there, here] = value.T


def unfold(core_at, own, other, width):
    whole = pl.BlockSpec(memory_space=pltpu.VMEM)
    return pl.pallas_call(
        unfold_kernel,
        in_specs=[pl.BlockSpec(memory_space=pltpu.SMEM), whole, whole],
        out_specs=whole,
        out_shape=jax.ShapeDtypeStruct((width, width), jnp.float32),
        compiler_params=pltpu.CompilerParams(vmem_limit_bytes=VMEM_BYTES),
        cost_estimate=pl.CostEstimate(flops=0, bytes_accessed=8 * own.size + 4 * width * width, transcendentals=0),
    )(core_at.reshape(1), own, other)


def shards(ancestor_inverse, panel, diag_inverse, inverse_pattern, panel_pattern):
    rows_count = lax.axis_size("row")
    cols_count = lax.axis_size("col")
    chips = cols_count // 2
    row_at = lax.axis_index("row")
    col_at = lax.axis_index("col")
    core_at = col_at % 2
    z_at = col_at // 2
    first = core_at == 0
    y_at, x_at = row_at // SIDE, row_at % SIDE
    phase_at = (jnp.where(first, x_at, y_at), jnp.where(first, y_at, x_at))
    block_rows, block_cols = ancestor_inverse.shape
    piece_rows, width = panel.shape
    half = width // 2
    slice_rows = half // rows_count
    inv_factor = jnp.tril(diag_inverse) + jnp.eye(width, dtype=jnp.float32)

    with jax.named_scope("local_scaled"):
        first_row = (row_at * cols_count + col_at) * piece_rows
        flags = lax.dynamic_slice(panel_pattern, (first_row // TILE, 0), (1, width // TILE))
        masked = panel * jnp.repeat(flags.astype(jnp.float32), TILE, axis=1)
        scaled = jnp.dot(masked, inv_factor, precision=HIGH)
    with jax.named_scope("gather_scaled"):
        left, right = scaled[:, :half], scaled[:, half:]
        mine = jnp.where(first, left, right)
        came = core_swap(jnp.where(first, right, left), cols_count)
        band_own = z_ring(by_core(first, mine, came, 0), cols_count)[0].reshape(block_rows, half)
        band_other = core_swap(band_own, cols_count)
    tile_at = jnp.stack([row_at * (block_rows // TILE), col_at * (block_cols // TILE)])

    turn = []
    for r in range(rows_count):
        for c in range(cols_count):
            y, x = divmod(r, SIDE)
            turn.append((r * cols_count + c, c * cols_count + (x * SIDE + y if c % 2 == 0 else r)))

    def sigma_slice(band):
        with jax.named_scope("product"):
            part = product(tile_at, inverse_pattern, band, ancestor_inverse)
        with jax.named_scope("sum_row"):
            for phase in range(2):
                part = plane_scatter(part, phase_at[phase], rows_count, cols_count, phase)
        return part

    own = sigma_slice(band_own)
    other = sigma_slice(band_other)
    with jax.named_scope("turn"):
        turned_own = lax.ppermute(own, BOTH, turn)
        turned_other = lax.ppermute(other, BOTH, turn)
    with jax.named_scope("sigma_out"):
        pieces = lax.all_to_all(pack(own, other, cols_count), "col", 0, 0)
        pieces = lax.all_to_all(pieces, "row", 0, 0)
        turned_own, turned_other, pieces = lax.optimization_barrier((turned_own, turned_other, pieces))
    with jax.named_scope("turn"):
        sigma_t = by_core(row_at % 2 == 0, turned_own, turned_other, 0)
    with jax.named_scope("quad"):
        quad = by_core(
            first,
            jnp.dot(sigma_t, band_own, precision=HIGH),
            jnp.dot(sigma_t, band_other, precision=HIGH),
            1,
        )
        share = width // rows_count
        factor_rows = lax.dynamic_slice(inv_factor, (row_at * share, 0), (share, width))
        factor_tile = jnp.concatenate(
            [
                lax.dynamic_slice(factor_rows, (0, part * half + col_at * slice_rows), (share, slice_rows))
                for part in range(2)
            ],
            axis=1,
        )
        base = lax.dot_general(factor_tile, factor_rows, (((0,), (0,)), ((), ())), precision=HIGH)
        term = base - quad
    with jax.named_scope("keep_half"):
        kept = width // 2 + LANES
        wrapped = jnp.concatenate([term, term[:, : width // 2]], axis=1)
        starts = [(part * half + col_at * slice_rows) // LANES * LANES for part in range(2)]
        term = jnp.concatenate(
            [
                lax.dynamic_slice(wrapped, (part * slice_rows, starts[part]), (slice_rows, kept))
                for part in range(2)
            ],
            axis=0,
        )
    with jax.named_scope("sum_diag"):
        term = plane_sum(term, rows_count, cols_count)
    with jax.named_scope("sigma_join"):
        sigma_panel = join(row_at % 2, pieces, piece_rows, width)
    with jax.named_scope("gather_diag"):
        held, sigma_panel = z_ring(term, cols_count, sigma_panel)
        sigma_diag = unfold(core_at, held, core_swap(held, cols_count), width)
    return sigma_panel, sigma_diag


def solution(mesh):
    return jax.shard_map(
        shards,
        mesh=mesh,
        in_specs=(P("row", "col"), P(("row", "col"), None), P(), P(), P()),
        out_specs=(P(("row", "col"), None), P()),
        check_vma=False,
    )
```

```python
import jax
import jax.numpy as jnp
from jax import lax
from jax.experimental import pallas as pl
from jax.experimental.pallas import tpu as pltpu
from jax.sharding import PartitionSpec as P

TILE = 256
SIDE = 4
LANES = 128
VMEM_BYTES = 16 * 1024 * 1024
BOTH = ("row", "col")
HIGH = lax.Precision.HIGH


def z_shift(cols_count, step):
    chips = cols_count // 2
    return [(z * 2 + k, ((z + step) % chips) * 2 + k) for z in range(chips) for k in range(2)]


def core_swap(value, cols_count):
    return lax.ppermute(value, "col", [(i, i ^ 1) for i in range(cols_count)])


def by_core(first, mine, other, axis):
    low, high = jnp.where(first, mine, other), jnp.where(first, other, mine)
    return jnp.concatenate([low, high], axis=axis)


def z_ring(piece, cols_count, beside=None):
    chips = cols_count // 2
    z_at = lax.axis_index("col") // 2
    held = jnp.zeros((chips,) + piece.shape, piece.dtype)
    held = lax.dynamic_update_slice(held, piece[None], (z_at, 0, 0))
    up = down = piece
    for step in range(1, chips // 2 + 1):
        if beside is not None and step == chips // 2 - 1:
            up, down, beside = lax.optimization_barrier((up, down, beside))
        up = lax.ppermute(up, "col", z_shift(cols_count, 1))
        held = lax.dynamic_update_slice(held, up[None], ((z_at - step) % chips, 0, 0))
        if step < chips // 2:
            down = lax.ppermute(down, "col", z_shift(cols_count, -1))
            held = lax.dynamic_update_slice(held, down[None], ((z_at + step) % chips, 0, 0))
    return held, beside


def plane_shift(rows_count, cols_count, step, phase):
    perm = []
    for r in range(rows_count):
        for c in range(cols_count):
            y, x = divmod(r, SIDE)
            if (c + phase) % 2 == 0:
                x = (x + step) % SIDE
            else:
                y = (y + step) % SIDE
            perm.append((r * cols_count + c, (y * SIDE + x) * cols_count + c))
    return perm


def plane_parts(value, at):
    parts = value.reshape((SIDE, value.shape[0] // SIDE) + value.shape[1:])
    return [lax.dynamic_index_in_dim(parts, (at + step) % SIDE, 0, keepdims=False) for step in range(SIDE)]


def plane_scatter(parts, rows_count, cols_count, phase):
    total = parts[0]
    for step in range(1, SIDE):
        total = total + lax.ppermute(parts[step], BOTH, plane_shift(rows_count, cols_count, step, phase))
    return total


def plane_sum(value, rows_count, cols_count):
    for phase in range(2):
        for bit in (1, 2):
            perm = []
            for r in range(rows_count):
                for c in range(cols_count):
                    other = r ^ (bit if (c + phase) % 2 == 0 else bit * SIDE)
                    perm.append((r * cols_count + c, other * cols_count + c))
            value = value + lax.ppermute(value, BOTH, perm)
    return value


def split(value):
    high = value.astype(jnp.bfloat16)
    return high, (value - high.astype(jnp.float32)).astype(jnp.bfloat16)


def product_kernel(at_ref, pattern_ref, band_ref, inverse_ref, *refs):
    out_refs, (high_ref, low_ref) = refs[:SIDE], refs[SIDE:]
    rows, cols = inverse_ref.shape
    part = band_ref.shape[1] // SIDE
    for q in range(SIDE):
        to = pl.ds(pl.multiple_of((q + SIDE - at_ref[2]) % SIDE * part, part), part)
        for i in range(rows // TILE):
            here = slice(i * TILE, (i + 1) * TILE)
            high, low = split(-band_ref[here, q * part : (q + 1) * part].T)
            high_ref[to, here] = high
            low_ref[to, here] = low
    for j in range(cols // TILE):
        there = slice(j * TILE, (j + 1) * TILE)
        masked = []
        for i in range(rows // TILE):
            flag = pattern_ref[at_ref[0] + i, at_ref[1] + j].astype(jnp.float32)
            masked.append(inverse_ref[i * TILE : (i + 1) * TILE, there] * flag)
        high, low = split(jnp.concatenate(masked, axis=0))
        total = jnp.dot(low_ref[...], high, preferred_element_type=jnp.float32)
        total += jnp.dot(high_ref[...], low, preferred_element_type=jnp.float32)
        total += jnp.dot(high_ref[...], high, preferred_element_type=jnp.float32)
        for q in range(SIDE):
            out_refs[q][:, there] = total[q * part : (q + 1) * part]


def product(at, pattern, band, inverse):
    rows, width = band.shape
    cols = inverse.shape[1]
    whole = pl.BlockSpec(memory_space=pltpu.VMEM)
    scalars = pl.BlockSpec(memory_space=pltpu.SMEM)
    return pl.pallas_call(
        product_kernel,
        in_specs=[scalars, scalars, whole, whole],
        out_specs=[whole] * SIDE,
        out_shape=[jax.ShapeDtypeStruct((width // SIDE, cols), jnp.float32)] * SIDE,
        scratch_shapes=[pltpu.VMEM((width, rows), jnp.bfloat16)] * 2,
        compiler_params=pltpu.CompilerParams(vmem_limit_bytes=VMEM_BYTES),
        cost_estimate=pl.CostEstimate(
            flops=6 * rows * width * cols, bytes_accessed=4 * (rows * width + rows * cols + width * cols), transcendentals=0
        ),
    )(at, pattern, band, inverse)


def pack_kernel(own_ref, other_ref, out_ref):
    piece = LANES // 2
    low = lax.broadcasted_iota(jnp.int32, (own_ref.shape[0], LANES), 1) < piece
    for pair in range(out_ref.shape[0] // 2):
        there = slice(pair * LANES, (pair + 1) * LANES)
        own, other = own_ref[:, there], other_ref[:, there]
        out_ref[2 * pair] = jnp.where(low, own, pltpu.roll(other, piece, 1))
        out_ref[2 * pair + 1] = jnp.where(low, pltpu.roll(own, piece, 1), other)


def pack(own, other, count):
    whole = pl.BlockSpec(memory_space=pltpu.VMEM)
    return pl.pallas_call(
        pack_kernel,
        in_specs=[whole, whole],
        out_specs=whole,
        out_shape=jax.ShapeDtypeStruct((count, own.shape[0], LANES), own.dtype),
        cost_estimate=pl.CostEstimate(flops=0, bytes_accessed=16 * own.size, transcendentals=0),
    )(own, other)


def join_kernel(odd_ref, pieces_ref, out_ref):
    even = odd_ref[0] == 0
    rows, width = out_ref.shape
    for x in range(SIDE):
        turned = jnp.concatenate([pieces_ref[x * SIDE + i] for i in range(SIDE)], axis=0).T
        own, other = turned[:rows], turned[rows:]
        out_ref[:, x * LANES : (x + 1) * LANES] = jnp.where(even, own, other)
        far = width // 2 + x * LANES
        out_ref[:, far : far + LANES] = jnp.where(even, other, own)


def join(odd, pieces, rows, width):
    return pl.pallas_call(
        join_kernel,
        in_specs=[pl.BlockSpec(memory_space=pltpu.SMEM), pl.BlockSpec(memory_space=pltpu.VMEM)],
        out_specs=pl.BlockSpec(memory_space=pltpu.VMEM),
        out_shape=jax.ShapeDtypeStruct((rows, width), pieces.dtype),
        cost_estimate=pl.CostEstimate(flops=0, bytes_accessed=8 * pieces.size, transcendentals=0),
    )(odd.reshape(1), pieces)


def unfold_kernel(core_ref, own_ref, other_ref, out_ref):
    chips, rows, kept = own_ref.shape
    part = rows // 2
    blocks = out_ref.shape[0] // LANES
    even = core_ref[0] == 0
    for block in range(blocks):
        at, chip = divmod(block, blocks // 2)
        chip = chip * (LANES // rows)
        strips = []
        for z in range(chip, chip + LANES // rows):
            own = own_ref[z, at * part : (at + 1) * part, :]
            other = other_ref[z, at * part : (at + 1) * part, :]
            strips += [jnp.where(even, own, other), jnp.where(even, other, own)]
        whole = jnp.concatenate(strips, axis=0)
        here = slice(block * LANES, (block + 1) * LANES)
        for step in range(kept // LANES):
            value = whole[:, step * LANES : (step + 1) * LANES]
            to = (block + step) % blocks
            there = slice(to * LANES, (to + 1) * LANES)
            out_ref[here, there] = value
            if 0 < step < blocks // 2:
                out_ref[there, here] = value.T


def unfold(core_at, own, other, width):
    whole = pl.BlockSpec(memory_space=pltpu.VMEM)
    return pl.pallas_call(
        unfold_kernel,
        in_specs=[pl.BlockSpec(memory_space=pltpu.SMEM), whole, whole],
        out_specs=whole,
        out_shape=jax.ShapeDtypeStruct((width, width), jnp.float32),
        compiler_params=pltpu.CompilerParams(vmem_limit_bytes=VMEM_BYTES),
        cost_estimate=pl.CostEstimate(flops=0, bytes_accessed=8 * own.size + 4 * width * width, transcendentals=0),
    )(core_at.reshape(1), own, other)


def shards(ancestor_inverse, panel, diag_inverse, inverse_pattern, panel_pattern):
    rows_count = lax.axis_size("row")
    cols_count = lax.axis_size("col")
    chips = cols_count // 2
    row_at = lax.axis_index("row")
    col_at = lax.axis_index("col")
    core_at = col_at % 2
    z_at = col_at // 2
    first = core_at == 0
    y_at, x_at = row_at // SIDE, row_at % SIDE
    phase_at = (jnp.where(first, x_at, y_at), jnp.where(first, y_at, x_at))
    block_rows, block_cols = ancestor_inverse.shape
    piece_rows, width = panel.shape
    half = width // 2
    slice_rows = half // rows_count
    inv_factor = jnp.tril(diag_inverse) + jnp.eye(width, dtype=jnp.float32)

    with jax.named_scope("local_scaled"):
        first_row = (row_at * cols_count + col_at) * piece_rows
        flags = lax.dynamic_slice(panel_pattern, (first_row // TILE, 0), (1, width // TILE))
        masked = panel * jnp.repeat(flags.astype(jnp.float32), TILE, axis=1)
        scaled = jnp.dot(masked, inv_factor, precision=HIGH)
    with jax.named_scope("gather_scaled"):
        left, right = scaled[:, :half], scaled[:, half:]
        mine = jnp.where(first, left, right)
        came = core_swap(jnp.where(first, right, left), cols_count)
        band_own = z_ring(by_core(first, mine, came, 0), cols_count)[0].reshape(block_rows, half)
        band_other = core_swap(band_own, cols_count)
    tile_at = jnp.stack([row_at * (block_rows // TILE), col_at * (block_cols // TILE), phase_at[0]])

    turn = []
    for r in range(rows_count):
        for c in range(cols_count):
            y, x = divmod(r, SIDE)
            turn.append((r * cols_count + c, c * cols_count + (x * SIDE + y if c % 2 == 0 else r)))

    def sigma_slice(band):
        with jax.named_scope("product"):
            parts = product(tile_at, inverse_pattern, band, ancestor_inverse)
        with jax.named_scope("sum_row"):
            part = plane_scatter(parts, rows_count, cols_count, 0)
            part = plane_scatter(plane_parts(part, phase_at[1]), rows_count, cols_count, 1)
        with jax.named_scope("turn"):
            return lax.ppermute(part, BOTH, turn)

    own = sigma_slice(band_own)
    other = sigma_slice(band_other)
    with jax.named_scope("sigma_out"):
        pieces = lax.all_to_all(pack(own, other, cols_count), "col", 0, 0)
    sigma_t = by_core(row_at % 2 == 0, own, other, 0)
    with jax.named_scope("quad"):
        quad = by_core(
            first,
            jnp.dot(sigma_t, band_own, precision=HIGH),
            jnp.dot(sigma_t, band_other, precision=HIGH),
            1,
        )
        share = width // rows_count
        factor_rows = lax.dynamic_slice(diag_inverse, (row_at * share, 0), (share, width))
        below = row_at * share + lax.broadcasted_iota(jnp.int32, (share, width), 0)
        below = below - lax.broadcasted_iota(jnp.int32, (share, width), 1)
        factor_rows = jnp.where(below >= 0, factor_rows, 0.0) + (below == 0).astype(jnp.float32)
        factor_tile = jnp.concatenate(
            [
                lax.dynamic_slice(factor_rows, (0, part * half + col_at * slice_rows), (share, slice_rows))
                for part in range(2)
            ],
            axis=1,
        )
        base = lax.dot_general(factor_tile, factor_rows, (((0,), (0,)), ((), ())), precision=HIGH)
        term = base - quad
    with jax.named_scope("keep_half"):
        kept = width // 2 + LANES
        wrapped = jnp.concatenate([term, term[:, : width // 2]], axis=1)
        starts = [(part * half + col_at * slice_rows) // LANES * LANES for part in range(2)]
        term = jnp.concatenate(
            [
                lax.dynamic_slice(wrapped, (part * slice_rows, starts[part]), (slice_rows, kept))
                for part in range(2)
            ],
            axis=0,
        )
    with jax.named_scope("sum_diag"):
        term = plane_sum(term, rows_count, cols_count)
    with jax.named_scope("sigma_join"):
        sigma_panel = join(row_at % 2, pieces, piece_rows, width)
    with jax.named_scope("gather_diag"):
        held, sigma_panel = z_ring(term, cols_count, sigma_panel)
        sigma_diag = unfold(core_at, held, core_swap(held, cols_count), width)
    return sigma_panel, sigma_diag


def solution(mesh):
    return jax.shard_map(
        shards,
        mesh=mesh,
        in_specs=(P("row", "col"), P(("row", "col"), None), P(), P(), P()),
        out_specs=(P(("row", "col"), None), P()),
        check_vma=False,
    )
```

```python
import jax
import jax.numpy as jnp
from jax import lax
from jax.experimental import pallas as pl
from jax.experimental.pallas import tpu as pltpu
from jax.sharding import PartitionSpec as P

TILE = 256
SIDE = 4
LANES = 128
VMEM_BYTES = 16 * 1024 * 1024
BOTH = ("row", "col")
HIGH = lax.Precision.HIGH


def z_shift(cols_count, step):
    chips = cols_count // 2
    return [(z * 2 + k, ((z + step) % chips) * 2 + k) for z in range(chips) for k in range(2)]


def core_swap(value, cols_count):
    return lax.ppermute(value, "col", [(i, i ^ 1) for i in range(cols_count)])


def by_core(first, mine, other, axis):
    low, high = jnp.where(first, mine, other), jnp.where(first, other, mine)
    return jnp.concatenate([low, high], axis=axis)


def z_ring(piece, cols_count):
    chips = cols_count // 2
    z_at = lax.axis_index("col") // 2
    held = jnp.zeros((chips,) + piece.shape, piece.dtype)
    held = lax.dynamic_update_slice(held, piece[None], (z_at, 0, 0))
    up = down = piece
    for step in range(1, chips // 2 + 1):
        up = lax.ppermute(up, "col", z_shift(cols_count, 1))
        held = lax.dynamic_update_slice(held, up[None], ((z_at - step) % chips, 0, 0))
        if step < chips // 2:
            down = lax.ppermute(down, "col", z_shift(cols_count, -1))
            held = lax.dynamic_update_slice(held, down[None], ((z_at + step) % chips, 0, 0))
    return held


def z_ring_deliver(piece, blocks, cols_count):
    chips = cols_count // 2
    z_at = lax.axis_index("col") // 2
    kept = piece.shape[1]
    ahead = jnp.concatenate([blocks, blocks], axis=1)
    ahead = lax.dynamic_slice(ahead, (0, z_at * LANES), blocks.shape)
    held = jnp.zeros((chips, piece.shape[0], LANES + kept), piece.dtype)

    def keep(held, moved, chip):
        held = lax.dynamic_update_slice(held, moved[None, :, :LANES], (chip, 0, 0))
        return lax.dynamic_update_slice(held, moved[None, :, -kept:], (chip, 0, LANES))

    up = jnp.concatenate([ahead[:, LANES : (chips // 2 + 1) * LANES], piece], axis=1)
    behind = [ahead[:, (chips - i) * LANES : (chips - i + 1) * LANES] for i in range(1, chips // 2)]
    down = jnp.concatenate(behind + [piece], axis=1)
    for step in range(1, chips // 2 + 1):
        up = lax.ppermute(up, "col", z_shift(cols_count, 1))
        if step < chips // 2:
            down = lax.ppermute(down, "col", z_shift(cols_count, -1))
        if step == 1:
            held = keep(held, jnp.concatenate([ahead[:, :LANES], piece], axis=1), z_at)
        held = keep(held, up, (z_at - step) % chips)
        up = up[:, LANES:]
        if step < chips // 2:
            held = keep(held, down, (z_at + step) % chips)
            down = down[:, LANES:]
    return held


def plane_shift(rows_count, cols_count, step, phase):
    perm = []
    for r in range(rows_count):
        for c in range(cols_count):
            y, x = divmod(r, SIDE)
            if (c + phase) % 2 == 0:
                x = (x + step) % SIDE
            else:
                y = (y + step) % SIDE
            perm.append((r * cols_count + c, (y * SIDE + x) * cols_count + c))
    return perm


def plane_parts(value, at):
    parts = value.reshape((SIDE, value.shape[0] // SIDE) + value.shape[1:])
    return [lax.dynamic_index_in_dim(parts, (at + step) % SIDE, 0, keepdims=False) for step in range(SIDE)]


def plane_scatter(parts, rows_count, cols_count, phase):
    total = parts[0]
    for step in range(1, SIDE):
        total = total + lax.ppermute(parts[step], BOTH, plane_shift(rows_count, cols_count, step, phase))
    return total


def plane_sum(value, rows_count, cols_count):
    for phase in range(2):
        for bit in (1, 2):
            perm = []
            for r in range(rows_count):
                for c in range(cols_count):
                    other = r ^ (bit if (c + phase) % 2 == 0 else bit * SIDE)
                    perm.append((r * cols_count + c, other * cols_count + c))
            value = value + lax.ppermute(value, BOTH, perm)
    return value


def split(value):
    high = value.astype(jnp.bfloat16)
    return high, (value - high.astype(jnp.float32)).astype(jnp.bfloat16)


def product_kernel(at_ref, pattern_ref, band_ref, inverse_ref, *refs):
    out_refs, (high_ref, low_ref, tiles_ref, arrived) = refs[:SIDE], refs[SIDE:]
    rows, cols = inverse_ref.shape
    copies = []
    for j in range(cols // TILE):
        there = slice(j * TILE, (j + 1) * TILE)
        copies.append(pltpu.make_async_copy(inverse_ref.at[:, there], tiles_ref.at[j], arrived.at[j]))
        copies[j].start()
    part = band_ref.shape[1] // SIDE
    for q in range(SIDE):
        to = pl.ds(pl.multiple_of((q + SIDE - at_ref[2]) % SIDE * part, part), part)
        for i in range(rows // TILE):
            here = slice(i * TILE, (i + 1) * TILE)
            high, low = split(-band_ref[here, q * part : (q + 1) * part].T)
            high_ref[to, here] = high
            low_ref[to, here] = low
    for j in range(cols // TILE):
        there = slice(j * TILE, (j + 1) * TILE)
        copies[j].wait()
        masked = []
        for i in range(rows // TILE):
            flag = pattern_ref[at_ref[0] + i, at_ref[1] + j].astype(jnp.float32)
            masked.append(tiles_ref[j, i * TILE : (i + 1) * TILE, :] * flag)
        high, low = split(jnp.concatenate(masked, axis=0))
        total = jnp.dot(low_ref[...], high, preferred_element_type=jnp.float32)
        total += jnp.dot(high_ref[...], low, preferred_element_type=jnp.float32)
        total += jnp.dot(high_ref[...], high, preferred_element_type=jnp.float32)
        for q in range(SIDE):
            out_refs[q][:, there] = total[q * part : (q + 1) * part]


def product(at, pattern, band, inverse):
    rows, width = band.shape
    cols = inverse.shape[1]
    whole = pl.BlockSpec(memory_space=pltpu.VMEM)
    scalars = pl.BlockSpec(memory_space=pltpu.SMEM)
    return pl.pallas_call(
        product_kernel,
        in_specs=[scalars, scalars, whole, pl.BlockSpec(memory_space=pl.ANY)],
        out_specs=[whole] * SIDE,
        out_shape=[jax.ShapeDtypeStruct((width // SIDE, cols), jnp.float32)] * SIDE,
        scratch_shapes=[pltpu.VMEM((width, rows), jnp.bfloat16)] * 2
        + [pltpu.VMEM((cols // TILE, rows, TILE), jnp.float32), pltpu.SemaphoreType.DMA((cols // TILE,))],
        compiler_params=pltpu.CompilerParams(vmem_limit_bytes=VMEM_BYTES),
        cost_estimate=pl.CostEstimate(
            flops=6 * rows * width * cols, bytes_accessed=4 * (rows * width + rows * cols + width * cols), transcendentals=0
        ),
    )(at, pattern, band, inverse)


def unfold_kernel(core_ref, own_ref, other_ref, diag_ref, panel_ref):
    chips, rows, whole = own_ref.shape
    part = rows // 2
    kept = whole - LANES
    blocks = diag_ref.shape[0] // LANES
    piece = panel_ref.shape[0]
    even = core_ref[0] == 0
    for block in range(blocks):
        at, chip = divmod(block, blocks // 2)
        chip = chip * (LANES // rows)
        strips = []
        for z in range(chip, chip + LANES // rows):
            own = own_ref[z, at * part : (at + 1) * part, :]
            other = other_ref[z, at * part : (at + 1) * part, :]
            strips += [jnp.where(even, own, other), jnp.where(even, other, own)]
        strip = jnp.concatenate(strips, axis=0)
        here = slice(block * LANES, (block + 1) * LANES)
        for step in range(kept // LANES):
            value = strip[:, (step + 1) * LANES : (step + 2) * LANES]
            to = (block + step) % blocks
            there = slice(to * LANES, (to + 1) * LANES)
            diag_ref[here, there] = value
            if 0 < step < blocks // 2:
                diag_ref[there, here] = value.T
        turned = strip[:, :LANES].T
        panel_ref[:, here] = jnp.where(even, turned[:piece], turned[piece:])


def unfold(core_at, own, other, rows, width):
    whole = pl.BlockSpec(memory_space=pltpu.VMEM)
    return pl.pallas_call(
        unfold_kernel,
        in_specs=[pl.BlockSpec(memory_space=pltpu.SMEM), whole, whole],
        out_specs=[whole, whole],
        out_shape=[
            jax.ShapeDtypeStruct((width, width), jnp.float32),
            jax.ShapeDtypeStruct((rows, width), jnp.float32),
        ],
        compiler_params=pltpu.CompilerParams(vmem_limit_bytes=VMEM_BYTES),
        cost_estimate=pl.CostEstimate(flops=0, bytes_accessed=8 * own.size + 4 * width * width, transcendentals=0),
    )(core_at.reshape(1), own, other)


def shards(ancestor_inverse, panel, diag_inverse, inverse_pattern, panel_pattern):
    rows_count = lax.axis_size("row")
    cols_count = lax.axis_size("col")
    chips = cols_count // 2
    row_at = lax.axis_index("row")
    col_at = lax.axis_index("col")
    core_at = col_at % 2
    z_at = col_at // 2
    first = core_at == 0
    y_at, x_at = row_at // SIDE, row_at % SIDE
    phase_at = (jnp.where(first, x_at, y_at), jnp.where(first, y_at, x_at))
    block_rows, block_cols = ancestor_inverse.shape
    piece_rows, width = panel.shape
    half = width // 2
    slice_rows = half // rows_count
    inv_factor = jnp.tril(diag_inverse) + jnp.eye(width, dtype=jnp.float32)

    with jax.named_scope("local_scaled"):
        first_row = (row_at * cols_count + col_at) * piece_rows
        flags = lax.dynamic_slice(panel_pattern, (first_row // TILE, 0), (1, width // TILE))
        masked = panel * jnp.repeat(flags.astype(jnp.float32), TILE, axis=1)
        scaled = jnp.dot(masked, inv_factor, precision=HIGH)
    with jax.named_scope("gather_scaled"):
        left, right = scaled[:, :half], scaled[:, half:]
        mine = jnp.where(first, left, right)
        came = core_swap(jnp.where(first, right, left), cols_count)
        band_own = z_ring(by_core(first, mine, came, 0), cols_count).reshape(block_rows, half)
        band_other = core_swap(band_own, cols_count)
    tile_at = jnp.stack([row_at * (block_rows // TILE), col_at * (block_cols // TILE), phase_at[0]])

    turn = []
    for r in range(rows_count):
        for c in range(cols_count):
            y, x = divmod(r, SIDE)
            turn.append((r * cols_count + c, c * cols_count + (x * SIDE + y if c % 2 == 0 else r)))

    def sigma_slice(band):
        with jax.named_scope("product"):
            parts = product(tile_at, inverse_pattern, band, ancestor_inverse)
        with jax.named_scope("sum_row"):
            part = plane_scatter(parts, rows_count, cols_count, 0)
            part = plane_scatter(plane_parts(part, phase_at[1]), rows_count, cols_count, 1)
        with jax.named_scope("turn"):
            return lax.ppermute(part, BOTH, turn)

    own = sigma_slice(band_own)
    other = sigma_slice(band_other)
    sigma_t = by_core(row_at % 2 == 0, own, other, 0)
    with jax.named_scope("quad"):
        quad = by_core(
            first,
            jnp.dot(sigma_t, band_own, precision=HIGH),
            jnp.dot(sigma_t, band_other, precision=HIGH),
            1,
        )
        share = width // rows_count
        factor_rows = lax.dynamic_slice(diag_inverse, (row_at * share, 0), (share, width))
        below = row_at * share + lax.broadcasted_iota(jnp.int32, (share, width), 0)
        below = below - lax.broadcasted_iota(jnp.int32, (share, width), 1)
        factor_rows = jnp.where(below >= 0, factor_rows, 0.0) + (below == 0).astype(jnp.float32)
        factor_tile = jnp.concatenate(
            [
                lax.dynamic_slice(factor_rows, (0, part * half + col_at * slice_rows), (share, slice_rows))
                for part in range(2)
            ],
            axis=1,
        )
        base = lax.dot_general(factor_tile, factor_rows, (((0,), (0,)), ((), ())), precision=HIGH)
        term = base - quad
    with jax.named_scope("keep_half"):
        kept = width // 2 + LANES
        wrapped = jnp.concatenate([term, term[:, : width // 2]], axis=1)
        starts = [(part * half + col_at * slice_rows) // LANES * LANES for part in range(2)]
        term = jnp.concatenate(
            [
                lax.dynamic_slice(wrapped, (part * slice_rows, starts[part]), (slice_rows, kept))
                for part in range(2)
            ],
            axis=0,
        )
    with jax.named_scope("sum_diag"):
        term = plane_sum(term, rows_count, cols_count)
    with jax.named_scope("gather_diag"):
        held = z_ring_deliver(term, sigma_t, cols_count)
        sigma_diag, sigma_panel = unfold(core_at, held, core_swap(held, cols_count), piece_rows, width)
    return sigma_panel, sigma_diag


def solution(mesh):
    return jax.shard_map(
        shards,
        mesh=mesh,
        in_specs=(P("row", "col"), P(("row", "col"), None), P(), P(), P()),
        out_specs=(P(("row", "col"), None), P()),
        check_vma=False,
    )
```

```python
import jax
import jax.numpy as jnp
from jax import lax
from jax.experimental import pallas as pl
from jax.experimental.pallas import tpu as pltpu
from jax.sharding import PartitionSpec as P

TILE = 256
SIDE = 4
LANES = 128
VMEM_BYTES = 16 * 1024 * 1024
BOTH = ("row", "col")
HIGH = lax.Precision.HIGH


def z_shift(cols_count, step):
    chips = cols_count // 2
    return [(z * 2 + k, ((z + step) % chips) * 2 + k) for z in range(chips) for k in range(2)]


def core_swap(value, cols_count):
    return lax.ppermute(value, "col", [(i, i ^ 1) for i in range(cols_count)])


def by_core(first, mine, other, axis):
    low, high = jnp.where(first, mine, other), jnp.where(first, other, mine)
    return jnp.concatenate([low, high], axis=axis)


def z_ring(piece, cols_count, beside):
    chips = cols_count // 2
    z_at = lax.axis_index("col") // 2
    held = jnp.zeros((chips,) + piece.shape, piece.dtype)
    held = lax.dynamic_update_slice(held, piece[None], (z_at, 0, 0))
    up = down = piece
    for step in range(1, chips // 2 + 1):
        if step == 3:
            up, down, beside = lax.optimization_barrier((up, down, beside))
        up = lax.ppermute(up, "col", z_shift(cols_count, 1))
        held = lax.dynamic_update_slice(held, up[None], ((z_at - step) % chips, 0, 0))
        if step < chips // 2:
            down = lax.ppermute(down, "col", z_shift(cols_count, -1))
            held = lax.dynamic_update_slice(held, down[None], ((z_at + step) % chips, 0, 0))
    return held, beside


def z_ring_deliver(piece, blocks, cols_count):
    chips = cols_count // 2
    z_at = lax.axis_index("col") // 2
    kept = piece.shape[1]
    ahead = jnp.concatenate([blocks, blocks], axis=1)
    ahead = lax.dynamic_slice(ahead, (0, z_at * LANES), blocks.shape)
    held = jnp.zeros((chips, piece.shape[0], LANES + kept), piece.dtype)

    def keep(held, moved, chip):
        held = lax.dynamic_update_slice(held, moved[None, :, :LANES], (chip, 0, 0))
        return lax.dynamic_update_slice(held, moved[None, :, -kept:], (chip, 0, LANES))

    up = jnp.concatenate([ahead[:, LANES : (chips // 2 + 1) * LANES], piece], axis=1)
    behind = [ahead[:, (chips - i) * LANES : (chips - i + 1) * LANES] for i in range(1, chips // 2)]
    down = jnp.concatenate(behind + [piece], axis=1)
    for step in range(1, chips // 2 + 1):
        up = lax.ppermute(up, "col", z_shift(cols_count, 1))
        if step < chips // 2:
            down = lax.ppermute(down, "col", z_shift(cols_count, -1))
        if step == 1:
            held = keep(held, jnp.concatenate([ahead[:, :LANES], piece], axis=1), z_at)
        held = keep(held, up, (z_at - step) % chips)
        up = up[:, LANES:]
        if step < chips // 2:
            held = keep(held, down, (z_at + step) % chips)
            down = down[:, LANES:]
    return held


def plane_shift(rows_count, cols_count, step, phase):
    perm = []
    for r in range(rows_count):
        for c in range(cols_count):
            y, x = divmod(r, SIDE)
            if (c + phase) % 2 == 0:
                x = (x + step) % SIDE
            else:
                y = (y + step) % SIDE
            perm.append((r * cols_count + c, (y * SIDE + x) * cols_count + c))
    return perm


def plane_parts(value, at):
    parts = value.reshape((SIDE, value.shape[0] // SIDE) + value.shape[1:])
    return [lax.dynamic_index_in_dim(parts, (at + step) % SIDE, 0, keepdims=False) for step in range(SIDE)]


def plane_scatter(parts, rows_count, cols_count, phase):
    total = parts[0]
    for step in range(1, SIDE):
        total = total + lax.ppermute(parts[step], BOTH, plane_shift(rows_count, cols_count, step, phase))
    return total


def plane_sum(value, rows_count, cols_count):
    for phase in range(2):
        for bit in (1, 2):
            perm = []
            for r in range(rows_count):
                for c in range(cols_count):
                    other = r ^ (bit if (c + phase) % 2 == 0 else bit * SIDE)
                    perm.append((r * cols_count + c, other * cols_count + c))
            value = value + lax.ppermute(value, BOTH, perm)
    return value


def split(value):
    high = value.astype(jnp.bfloat16)
    return high, (value - high.astype(jnp.float32)).astype(jnp.bfloat16)


def prepare_kernel(at_ref, pattern_ref, inverse_ref, high_ref, low_ref):
    rows, cols = inverse_ref.shape
    for i in range(rows // TILE):
        for j in range(cols // TILE):
            here, there = slice(i * TILE, (i + 1) * TILE), slice(j * TILE, (j + 1) * TILE)
            flag = pattern_ref[at_ref[0] + i, at_ref[1] + j].astype(jnp.float32)
            high_ref[here, there], low_ref[here, there] = split(inverse_ref[here, there] * flag)


def prepare(at, pattern, inverse):
    whole = pl.BlockSpec(memory_space=pltpu.VMEM)
    scalars = pl.BlockSpec(memory_space=pltpu.SMEM)
    return pl.pallas_call(
        prepare_kernel,
        in_specs=[scalars, scalars, whole],
        out_specs=[whole] * 2,
        out_shape=[jax.ShapeDtypeStruct(inverse.shape, jnp.bfloat16)] * 2,
        compiler_params=pltpu.CompilerParams(vmem_limit_bytes=VMEM_BYTES),
        cost_estimate=pl.CostEstimate(flops=4 * inverse.size, bytes_accessed=8 * inverse.size, transcendentals=0),
    )(at, pattern, inverse)


def product_kernel(at_ref, band_ref, inverse_high_ref, inverse_low_ref, *refs):
    out_refs, (high_ref, low_ref) = refs[:SIDE], refs[SIDE:]
    rows, cols = inverse_high_ref.shape
    part = band_ref.shape[1] // SIDE
    for q in range(SIDE):
        to = pl.ds(pl.multiple_of((q + SIDE - at_ref[2]) % SIDE * part, part), part)
        for i in range(rows // TILE):
            here = slice(i * TILE, (i + 1) * TILE)
            high, low = split(-band_ref[here, q * part : (q + 1) * part].T)
            high_ref[to, here] = high
            low_ref[to, here] = low
    for j in range(cols // TILE):
        there = slice(j * TILE, (j + 1) * TILE)
        high = inverse_high_ref[:, there]
        total = jnp.dot(low_ref[...], high, preferred_element_type=jnp.float32)
        total += jnp.dot(high_ref[...], inverse_low_ref[:, there], preferred_element_type=jnp.float32)
        total += jnp.dot(high_ref[...], high, preferred_element_type=jnp.float32)
        for q in range(SIDE):
            out_refs[q][:, there] = total[q * part : (q + 1) * part]


def product(at, band, high, low):
    rows, width = band.shape
    cols = high.shape[1]
    whole = pl.BlockSpec(memory_space=pltpu.VMEM)
    return pl.pallas_call(
        product_kernel,
        in_specs=[pl.BlockSpec(memory_space=pltpu.SMEM), whole, whole, whole],
        out_specs=[whole] * SIDE,
        out_shape=[jax.ShapeDtypeStruct((width // SIDE, cols), jnp.float32)] * SIDE,
        scratch_shapes=[pltpu.VMEM((width, rows), jnp.bfloat16)] * 2,
        compiler_params=pltpu.CompilerParams(vmem_limit_bytes=VMEM_BYTES),
        cost_estimate=pl.CostEstimate(
            flops=6 * rows * width * cols, bytes_accessed=4 * (rows * width + rows * cols + width * cols), transcendentals=0
        ),
    )(at, band, high, low)


def unfold_kernel(core_ref, own_ref, other_ref, diag_ref, panel_ref):
    chips, rows, whole = own_ref.shape
    part = rows // 2
    kept = whole - LANES
    blocks = diag_ref.shape[0] // LANES
    piece = panel_ref.shape[0]
    even = core_ref[0] == 0
    for block in range(blocks):
        at, chip = divmod(block, blocks // 2)
        chip = chip * (LANES // rows)
        strips = []
        for z in range(chip, chip + LANES // rows):
            own = own_ref[z, at * part : (at + 1) * part, :]
            other = other_ref[z, at * part : (at + 1) * part, :]
            strips += [jnp.where(even, own, other), jnp.where(even, other, own)]
        strip = jnp.concatenate(strips, axis=0)
        here = slice(block * LANES, (block + 1) * LANES)
        for step in range(kept // LANES):
            value = strip[:, (step + 1) * LANES : (step + 2) * LANES]
            to = (block + step) % blocks
            there = slice(to * LANES, (to + 1) * LANES)
            diag_ref[here, there] = value
            if 0 < step < blocks // 2:
                diag_ref[there, here] = value.T
        turned = strip[:, :LANES].T
        panel_ref[:, here] = jnp.where(even, turned[:piece], turned[piece:])


def unfold(core_at, own, other, rows, width):
    whole = pl.BlockSpec(memory_space=pltpu.VMEM)
    return pl.pallas_call(
        unfold_kernel,
        in_specs=[pl.BlockSpec(memory_space=pltpu.SMEM), whole, whole],
        out_specs=[whole, whole],
        out_shape=[
            jax.ShapeDtypeStruct((width, width), jnp.float32),
            jax.ShapeDtypeStruct((rows, width), jnp.float32),
        ],
        compiler_params=pltpu.CompilerParams(vmem_limit_bytes=VMEM_BYTES),
        cost_estimate=pl.CostEstimate(flops=0, bytes_accessed=8 * own.size + 4 * width * width, transcendentals=0),
    )(core_at.reshape(1), own, other)


def shards(ancestor_inverse, panel, diag_inverse, inverse_pattern, panel_pattern):
    rows_count = lax.axis_size("row")
    cols_count = lax.axis_size("col")
    chips = cols_count // 2
    row_at = lax.axis_index("row")
    col_at = lax.axis_index("col")
    core_at = col_at % 2
    z_at = col_at // 2
    first = core_at == 0
    y_at, x_at = row_at // SIDE, row_at % SIDE
    phase_at = (
        (jnp.where(first, x_at, y_at) - col_at // SIDE) % SIDE,
        (jnp.where(first, y_at, x_at) - col_at % SIDE) % SIDE,
    )
    block_rows, block_cols = ancestor_inverse.shape
    piece_rows, width = panel.shape
    half = width // 2
    slice_rows = half // rows_count
    inv_factor = jnp.tril(diag_inverse) + jnp.eye(width, dtype=jnp.float32)

    tile_at = jnp.stack([row_at * (block_rows // TILE), col_at * (block_cols // TILE), phase_at[0]])
    with jax.named_scope("prepare_inverse"):
        prepared = prepare(tile_at, inverse_pattern, ancestor_inverse)
    with jax.named_scope("local_scaled"):
        first_row = (row_at * cols_count + col_at) * piece_rows
        flags = lax.dynamic_slice(panel_pattern, (first_row // TILE, 0), (1, width // TILE))
        masked = panel * jnp.repeat(flags.astype(jnp.float32), TILE, axis=1)
        scaled = jnp.dot(masked, inv_factor, precision=HIGH)
    with jax.named_scope("gather_scaled"):
        left, right = scaled[:, :half], scaled[:, half:]
        mine = jnp.where(first, left, right)
        came = core_swap(jnp.where(first, right, left), cols_count)
        band_own, prepared = z_ring(by_core(first, mine, came, 0), cols_count, prepared)
        band_own = band_own.reshape(block_rows, half)
        band_other = core_swap(band_own, cols_count)
    turn = []
    for r in range(rows_count):
        for c in range(cols_count):
            y, x = divmod(r, SIDE)
            at = (x, y) if c % 2 == 0 else (y, x)
            slot = (at[0] - c // SIDE) % SIDE * SIDE + (at[1] - c % SIDE) % SIDE
            turn.append((r * cols_count + c, c * cols_count + slot))

    def sigma_slice(band):
        with jax.named_scope("product"):
            parts = product(tile_at, band, *prepared)
        with jax.named_scope("sum_row"):
            part = plane_scatter(parts, rows_count, cols_count, 0)
            part = plane_scatter(plane_parts(part, phase_at[1]), rows_count, cols_count, 1)
        with jax.named_scope("turn"):
            return lax.ppermute(part, BOTH, turn)

    own = sigma_slice(band_own)
    other = sigma_slice(band_other)
    sigma_t = by_core(row_at % 2 == 0, own, other, 0)
    with jax.named_scope("quad"):
        quad = by_core(
            first,
            jnp.dot(sigma_t, band_own, precision=HIGH),
            jnp.dot(sigma_t, band_other, precision=HIGH),
            1,
        )
        share = width // rows_count
        factor_rows = lax.dynamic_slice(diag_inverse, (row_at * share, 0), (share, width))
        below = row_at * share + lax.broadcasted_iota(jnp.int32, (share, width), 0)
        below = below - lax.broadcasted_iota(jnp.int32, (share, width), 1)
        factor_rows = jnp.where(below >= 0, factor_rows, 0.0) + (below == 0).astype(jnp.float32)
        factor_tile = jnp.concatenate(
            [
                lax.dynamic_slice(factor_rows, (0, part * half + col_at * slice_rows), (share, slice_rows))
                for part in range(2)
            ],
            axis=1,
        )
        base = lax.dot_general(factor_tile, factor_rows, (((0,), (0,)), ((), ())), precision=HIGH)
        term = base - quad
    with jax.named_scope("keep_half"):
        kept = width // 2 + LANES
        wrapped = jnp.concatenate([term, term[:, : width // 2]], axis=1)
        starts = [(part * half + col_at * slice_rows) // LANES * LANES for part in range(2)]
        term = jnp.concatenate(
            [
                lax.dynamic_slice(wrapped, (part * slice_rows, starts[part]), (slice_rows, kept))
                for part in range(2)
            ],
            axis=0,
        )
    with jax.named_scope("sum_diag"):
        term = plane_sum(term, rows_count, cols_count)
    with jax.named_scope("gather_diag"):
        held = z_ring_deliver(term, sigma_t, cols_count)
        sigma_diag, sigma_panel = unfold(core_at, held, core_swap(held, cols_count), piece_rows, width)
    return sigma_panel, sigma_diag


def solution(mesh):
    return jax.shard_map(
        shards,
        mesh=mesh,
        in_specs=(P("row", "col"), P(("row", "col"), None), P(), P(), P()),
        out_specs=(P(("row", "col"), None), P()),
        check_vma=False,
    )
```

```python
import jax
import jax.numpy as jnp
from jax import lax
from jax.experimental import pallas as pl
from jax.experimental.pallas import tpu as pltpu
from jax.sharding import PartitionSpec as P

TILE = 256
SIDE = 4
LANES = 128
VMEM_BYTES = 16 * 1024 * 1024
BOTH = ("row", "col")
HIGH = lax.Precision.HIGH


def z_shift(cols_count, step):
    chips = cols_count // 2
    return [(z * 2 + k, ((z + step) % chips) * 2 + k) for z in range(chips) for k in range(2)]


def core_swap(value, cols_count):
    return lax.ppermute(value, "col", [(i, i ^ 1) for i in range(cols_count)])


def by_core(first, mine, other, axis):
    low, high = jnp.where(first, mine, other), jnp.where(first, other, mine)
    return jnp.concatenate([low, high], axis=axis)


def z_ring(piece, cols_count, beside):
    chips = cols_count // 2
    z_at = lax.axis_index("col") // 2
    held = jnp.zeros((chips,) + piece.shape, piece.dtype)
    held = lax.dynamic_update_slice(held, piece[None], (z_at, 0, 0))
    up = down = piece
    for step in range(1, chips // 2):
        if step == 3:
            up, down, beside = lax.optimization_barrier((up, down, beside))
        up = lax.ppermute(up, "col", z_shift(cols_count, 1))
        held = lax.dynamic_update_slice(held, up[None], ((z_at - step) % chips, 0, 0))
        down = lax.ppermute(down, "col", z_shift(cols_count, -1))
        held = lax.dynamic_update_slice(held, down[None], ((z_at + step) % chips, 0, 0))
    middle = piece.shape[0] // 2
    up = lax.ppermute(up[:middle], "col", z_shift(cols_count, 1))
    held = lax.dynamic_update_slice(held, up[None], ((z_at - chips // 2) % chips, 0, 0))
    down = lax.ppermute(down[middle:], "col", z_shift(cols_count, -1))
    held = lax.dynamic_update_slice(held, down[None], ((z_at + chips // 2) % chips, middle, 0))
    return held, beside


def z_ring_deliver(piece, blocks, cols_count):
    chips = cols_count // 2
    z_at = lax.axis_index("col") // 2
    rows, kept = blocks.shape[1], piece.shape[0]
    ahead = lax.dynamic_slice(jnp.concatenate([blocks, blocks], axis=0), (z_at, 0, 0), blocks.shape)
    held = jnp.zeros((chips, rows + kept, LANES), piece.dtype)

    def keep(held, moved, chip):
        moved = jnp.concatenate([moved[:rows], moved[-kept:]], axis=0)
        return lax.dynamic_update_slice(held, moved[None], (chip, 0, 0))

    up = jnp.concatenate([ahead[i] for i in range(1, chips // 2 + 1)] + [piece], axis=0)
    down = jnp.concatenate([ahead[chips - i] for i in range(1, chips // 2)] + [piece], axis=0)
    for step in range(1, chips // 2 + 1):
        up = lax.ppermute(up, "col", z_shift(cols_count, 1))
        if step < chips // 2:
            down = lax.ppermute(down, "col", z_shift(cols_count, -1))
        if step == 1:
            held = keep(held, jnp.concatenate([ahead[0], piece], axis=0), z_at)
        held = keep(held, up, (z_at - step) % chips)
        up = up[rows:]
        if step < chips // 2:
            held = keep(held, down, (z_at + step) % chips)
            down = down[rows:]
    return held


def plane_shift(rows_count, cols_count, step, phase):
    perm = []
    for r in range(rows_count):
        for c in range(cols_count):
            y, x = divmod(r, SIDE)
            if (c + phase) % 2 == 0:
                x = (x + step) % SIDE
            else:
                y = (y + step) % SIDE
            perm.append((r * cols_count + c, (y * SIDE + x) * cols_count + c))
    return perm


def plane_parts(value, at):
    parts = value.reshape((SIDE, value.shape[0] // SIDE) + value.shape[1:])
    return [lax.dynamic_index_in_dim(parts, (at + step) % SIDE, 0, keepdims=False) for step in range(SIDE)]


def plane_scatter(parts, rows_count, cols_count, phase):
    total = parts[0]
    for step in range(1, SIDE):
        total = total + lax.ppermute(parts[step], BOTH, plane_shift(rows_count, cols_count, step, phase))
    return total


def plane_sum(value, rows_count, cols_count, phase):
    one, two, three = [
        lax.ppermute(value, BOTH, plane_shift(rows_count, cols_count, step, phase)) for step in range(1, SIDE)
    ]
    return (value + two) + (one + three)


def plane_gather(value, rows_count, cols_count, phase):
    return [value] + [
        lax.ppermute(value, BOTH, plane_shift(rows_count, cols_count, step, phase)) for step in range(1, SIDE)
    ]


def split(value):
    high = value.astype(jnp.bfloat16)
    return high, (value - high.astype(jnp.float32)).astype(jnp.bfloat16)


def prepare_kernel(at_ref, pattern_ref, inverse_ref, high_ref, low_ref):
    rows, cols = inverse_ref.shape
    for i in range(rows // TILE):
        for j in range(cols // TILE):
            here, there = slice(i * TILE, (i + 1) * TILE), slice(j * TILE, (j + 1) * TILE)
            flag = pattern_ref[at_ref[0] + i, at_ref[1] + j].astype(jnp.float32)
            high_ref[here, there], low_ref[here, there] = split(inverse_ref[here, there] * flag)


def prepare(at, pattern, inverse):
    whole = pl.BlockSpec(memory_space=pltpu.VMEM)
    scalars = pl.BlockSpec(memory_space=pltpu.SMEM)
    return pl.pallas_call(
        prepare_kernel,
        in_specs=[scalars, scalars, whole],
        out_specs=[whole] * 2,
        out_shape=[jax.ShapeDtypeStruct(inverse.shape, jnp.bfloat16)] * 2,
        compiler_params=pltpu.CompilerParams(vmem_limit_bytes=VMEM_BYTES),
        cost_estimate=pl.CostEstimate(flops=4 * inverse.size, bytes_accessed=8 * inverse.size, transcendentals=0),
    )(at, pattern, inverse)


def product_kernel(at_ref, band_ref, inverse_high_ref, inverse_low_ref, *refs):
    out_refs, (high_ref, low_ref) = refs[:SIDE], refs[-2:]
    rows, cols = inverse_high_ref.shape
    part = band_ref.shape[1] // SIDE
    for q in range(SIDE):
        to = pl.ds(pl.multiple_of((q + SIDE - at_ref[2]) % SIDE * part, part), part)
        for i in range(rows // TILE):
            here = slice(i * TILE, (i + 1) * TILE)
            high, low = split(-band_ref[here, q * part : (q + 1) * part].T)
            high_ref[to, here] = high
            low_ref[to, here] = low
    for j in range(cols // TILE):
        there = slice(j * TILE, (j + 1) * TILE)
        high = inverse_high_ref[:, there]
        total = jnp.dot(low_ref[...], high, preferred_element_type=jnp.float32)
        total += jnp.dot(high_ref[...], inverse_low_ref[:, there], preferred_element_type=jnp.float32)
        total += jnp.dot(high_ref[...], high, preferred_element_type=jnp.float32)
        for q in range(SIDE):
            out_refs[q][:, there] = total[q * part : (q + 1) * part]


def product(at, band, high, low):
    rows, width = band.shape
    cols = high.shape[1]
    whole = pl.BlockSpec(memory_space=pltpu.VMEM)
    return pl.pallas_call(
        product_kernel,
        in_specs=[pl.BlockSpec(memory_space=pltpu.SMEM), whole, whole, whole],
        out_specs=[whole] * SIDE,
        out_shape=[jax.ShapeDtypeStruct((width // SIDE, cols), jnp.float32)] * SIDE,
        scratch_shapes=[pltpu.VMEM((width, rows), jnp.bfloat16)] * 2,
        compiler_params=pltpu.CompilerParams(vmem_limit_bytes=VMEM_BYTES),
        cost_estimate=pl.CostEstimate(
            flops=6 * rows * width * cols, bytes_accessed=4 * (rows * width + rows * cols + width * cols), transcendentals=0
        ),
    )(at, band, high, low)


def unfold_kernel(at_ref, *refs):
    parts, (own_block_ref, other_block_ref, diag_ref, panel_ref, own_ref, other_ref) = refs[:-6], refs[-6:]
    sides, chips, kept, _ = own_ref.shape
    for step in range(sides):
        own_ref[(at_ref[1] + sides - step) % sides] = parts[step][...]
        other_ref[(at_ref[2] + sides - step) % sides] = parts[sides + step][...]
    blocks = diag_ref.shape[0] // LANES
    steps = blocks // 2 + 1
    rows = kept // steps
    part = own_block_ref.shape[1] // 2
    piece = panel_ref.shape[0]
    even = at_ref[0] == 0

    def both(own, other):
        return [jnp.where(even, own, other), jnp.where(even, other, own)]

    for block in range(blocks):
        at, chip = divmod(block, blocks // 2)
        chip = chip * (LANES // (2 * part))
        here = slice(block * LANES, (block + 1) * LANES)
        for step in range(steps):
            strips = []
            for z in range(chip, chip + LANES // (2 * part)):
                sources = []
                for ref in (own_ref, other_ref):
                    quarters = [
                        ref[q, z, step * rows : (step + 1) * rows, :]
                        for q in range(at * sides // 2, (at + 1) * sides // 2)
                    ]
                    sources.append(jnp.concatenate(quarters, axis=0))
                strips += both(*sources)
            value = jnp.concatenate(strips, axis=0)
            to = (block + step) % blocks
            there = slice(to * LANES, (to + 1) * LANES)
            diag_ref[here, there] = value
            if 0 < step < blocks // 2:
                diag_ref[there, here] = value.T
        strips = []
        for z in range(chip, chip + LANES // (2 * part)):
            strips += both(*[ref[z, at * part : (at + 1) * part, :] for ref in (own_block_ref, other_block_ref)])
        turned = jnp.concatenate(strips, axis=0).T
        panel_ref[:, here] = jnp.where(even, turned[:piece], turned[piece:])


def unfold(at, own, other, own_block, other_block, rows, width):
    whole = pl.BlockSpec(memory_space=pltpu.VMEM)
    held = pltpu.VMEM((SIDE,) + own[0].shape, jnp.float32)
    return pl.pallas_call(
        unfold_kernel,
        in_specs=[pl.BlockSpec(memory_space=pltpu.SMEM)] + [whole] * (2 * SIDE + 2),
        out_specs=[whole, whole],
        out_shape=[
            jax.ShapeDtypeStruct((width, width), jnp.float32),
            jax.ShapeDtypeStruct((rows, width), jnp.float32),
        ],
        scratch_shapes=[held, held],
        compiler_params=pltpu.CompilerParams(vmem_limit_bytes=VMEM_BYTES),
        cost_estimate=pl.CostEstimate(
            flops=0, bytes_accessed=16 * SIDE * own[0].size + 4 * width * width, transcendentals=0
        ),
    )(at, *own, *other, own_block, other_block)


def shards(ancestor_inverse, panel, diag_inverse, inverse_pattern, panel_pattern):
    rows_count = lax.axis_size("row")
    cols_count = lax.axis_size("col")
    chips = cols_count // 2
    row_at = lax.axis_index("row")
    col_at = lax.axis_index("col")
    core_at = col_at % 2
    z_at = col_at // 2
    first = core_at == 0
    y_at, x_at = row_at // SIDE, row_at % SIDE
    phase_at = (
        (jnp.where(first, x_at, y_at) - col_at // SIDE) % SIDE,
        (jnp.where(first, y_at, x_at) - col_at % SIDE) % SIDE,
    )
    block_rows, block_cols = ancestor_inverse.shape
    piece_rows, width = panel.shape
    half = width // 2
    slice_rows = half // rows_count
    inv_factor = jnp.tril(diag_inverse) + jnp.eye(width, dtype=jnp.float32)

    tile_at = jnp.stack([row_at * (block_rows // TILE), col_at * (block_cols // TILE), phase_at[0]])
    with jax.named_scope("prepare_inverse"):
        prepared = prepare(tile_at, inverse_pattern, ancestor_inverse)
    with jax.named_scope("local_scaled"):
        first_row = (row_at * cols_count + col_at) * piece_rows
        flags = lax.dynamic_slice(panel_pattern, (first_row // TILE, 0), (1, width // TILE))
        masked = panel * jnp.repeat(flags.astype(jnp.float32), TILE, axis=1)
        scaled = jnp.dot(masked, inv_factor, precision=HIGH)
    with jax.named_scope("gather_scaled"):
        left, right = scaled[:, :half], scaled[:, half:]
        mine = jnp.where(first, left, right)
        came = core_swap(jnp.where(first, right, left), cols_count)
        band_own, prepared = z_ring(by_core(first, mine, came, 0), cols_count, prepared)
        band_own = band_own.reshape(block_rows, half)
        band_other = core_swap(band_own, cols_count)
    turn = []
    for r in range(rows_count):
        for c in range(cols_count):
            y, x = divmod(r, SIDE)
            at = (x, y) if c % 2 == 0 else (y, x)
            slot = (at[0] - c // SIDE) % SIDE * SIDE + (at[1] - c % SIDE) % SIDE
            turn.append((r * cols_count + c, c * cols_count + slot))

    def sigma_slice(band):
        with jax.named_scope("product"):
            parts = product(tile_at, band, *prepared)
        with jax.named_scope("sum_row"):
            part = plane_scatter(parts, rows_count, cols_count, 0)
            part = plane_scatter(plane_parts(part, phase_at[1]), rows_count, cols_count, 1)
        with jax.named_scope("turn"):
            return lax.ppermute(part, BOTH, turn)

    own = sigma_slice(band_own)
    other = sigma_slice(band_other)
    sigma_t = by_core(row_at % 2 == 0, own, other, 0)
    with jax.named_scope("quad"):
        quad = by_core(
            first,
            jnp.dot(sigma_t, band_own, precision=HIGH),
            jnp.dot(sigma_t, band_other, precision=HIGH),
            1,
        )
        share = width // rows_count
        factor_rows = lax.dynamic_slice(diag_inverse, (row_at * share, 0), (share, width))
        below = row_at * share + lax.broadcasted_iota(jnp.int32, (share, width), 0)
        below = below - lax.broadcasted_iota(jnp.int32, (share, width), 1)
        factor_rows = jnp.where(below >= 0, factor_rows, 0.0) + (below == 0).astype(jnp.float32)
        factor_tile = jnp.concatenate(
            [
                lax.dynamic_slice(factor_rows, (0, part * half + col_at * slice_rows), (share, slice_rows))
                for part in range(2)
            ],
            axis=1,
        )
        base = lax.dot_general(factor_tile, factor_rows, (((0,), (0,)), ((), ())), precision=HIGH)
        term = base - quad
    with jax.named_scope("keep_half"):
        kept = width // 2 + LANES
        wrapped = jnp.concatenate([term, term[:, : width // 2]], axis=1)
        starts = [(part * half + col_at * slice_rows) // LANES * LANES for part in range(2)]
        term = jnp.concatenate(
            [
                lax.dynamic_slice(wrapped, (part * slice_rows, starts[part]), (slice_rows, kept))
                for part in range(2)
            ],
            axis=0,
        )
    with jax.named_scope("sum_diag"):
        axis_at = jnp.where(first, x_at, y_at)
        term = plane_scatter(plane_parts(term, axis_at), rows_count, cols_count, 0)
        term = plane_sum(term, rows_count, cols_count, 1)
        term = jnp.concatenate([term[:, at : at + LANES] for at in range(0, kept, LANES)], axis=0)
    with jax.named_scope("gather_diag"):
        blocks = jnp.stack([sigma_t[:, at : at + LANES] for at in range(0, block_cols, LANES)])
        held = z_ring_deliver(term, blocks, cols_count)
        block = held[:, : 2 * slice_rows]
        other_block = core_swap(block, cols_count)
        parts = plane_gather(held[:, 2 * slice_rows :], rows_count, cols_count, 0)
        other_parts = [core_swap(part, cols_count) for part in parts]
        places = jnp.stack([core_at, axis_at, jnp.where(first, y_at, x_at)])
        sigma_diag, sigma_panel = unfold(places, parts, other_parts, block, other_block, piece_rows, width)
    return sigma_panel, sigma_diag


def solution(mesh):
    return jax.shard_map(
        shards,
        mesh=mesh,
        in_specs=(P("row", "col"), P(("row", "col"), None), P(), P(), P()),
        out_specs=(P(("row", "col"), None), P()),
        check_vma=False,
    )
```

```python
import jax
import jax.numpy as jnp
from jax import lax
from jax.experimental import pallas as pl
from jax.experimental.pallas import tpu as pltpu
from jax.sharding import PartitionSpec as P

TILE = 256
SIDE = 4
LANES = 128
VMEM_BYTES = 16 * 1024 * 1024
BOTH = ("row", "col")
HIGH = lax.Precision.HIGH


def z_shift(cols_count, step):
    chips = cols_count // 2
    return [(z * 2 + k, ((z + step) % chips) * 2 + k) for z in range(chips) for k in range(2)]


def core_swap(value, cols_count):
    return lax.ppermute(value, "col", [(i, i ^ 1) for i in range(cols_count)])


def by_core(first, mine, other, axis):
    low, high = jnp.where(first, mine, other), jnp.where(first, other, mine)
    return jnp.concatenate([low, high], axis=axis)


def z_ring(piece, cols_count, beside):
    chips = cols_count // 2
    z_at = lax.axis_index("col") >> 1
    held = jnp.zeros((chips,) + piece.shape, piece.dtype)
    held = lax.dynamic_update_slice(held, piece[None], (z_at, 0, 0))
    up = down = piece
    for step in range(1, chips // 2):
        if step == 3:
            up, down, beside = lax.optimization_barrier((up, down, beside))
        up = lax.ppermute(up, "col", z_shift(cols_count, 1))
        held = lax.dynamic_update_slice(held, up[None], ((z_at - step) & (chips - 1), 0, 0))
        down = lax.ppermute(down, "col", z_shift(cols_count, -1))
        held = lax.dynamic_update_slice(held, down[None], ((z_at + step) & (chips - 1), 0, 0))
    up = lax.ppermute(up, "col", z_shift(cols_count, 1))
    held = lax.dynamic_update_slice(held, up[None], ((z_at - chips // 2) & (chips - 1), 0, 0))
    return held, beside


def z_ring_deliver(piece, blocks, cols_count):
    chips = cols_count // 2
    z_at = lax.axis_index("col") >> 1
    rows, kept = blocks.shape[0], piece.shape[0]
    ahead = lax.dynamic_slice(jnp.concatenate([blocks, blocks], axis=1), (0, z_at * LANES), blocks.shape)
    ahead = ahead.reshape(rows, chips, LANES).transpose(1, 0, 2)
    held = jnp.zeros((chips, rows + kept, LANES), piece.dtype)

    def keep(held, moved, chip):
        moved = jnp.concatenate([moved[:rows], moved[-kept:]], axis=0)
        return lax.dynamic_update_slice(held, moved[None], (chip, 0, 0))

    up = jnp.concatenate([ahead[1 : chips // 2 + 1].reshape(-1, LANES), piece], axis=0)
    down = jnp.concatenate([ahead[: chips // 2 : -1].reshape(-1, LANES), piece], axis=0)
    for step in range(1, chips // 2 + 1):
        up = lax.ppermute(up, "col", z_shift(cols_count, 1))
        if step < chips // 2:
            down = lax.ppermute(down, "col", z_shift(cols_count, -1))
        if step == 1:
            held = keep(held, jnp.concatenate([ahead[0], piece], axis=0), z_at)
        held = keep(held, up, (z_at - step) & (chips - 1))
        up = up[rows:]
        if step < chips // 2:
            held = keep(held, down, (z_at + step) & (chips - 1))
            down = down[rows:]
    return held


def plane_shift(rows_count, cols_count, step, phase):
    perm = []
    for r in range(rows_count):
        for c in range(cols_count):
            y, x = divmod(r, SIDE)
            if (c + phase) % 2 == 0:
                x = (x + step) % SIDE
            else:
                y = (y + step) % SIDE
            perm.append((r * cols_count + c, (y * SIDE + x) * cols_count + c))
    return perm


def plane_parts(value, at):
    parts = value.reshape((SIDE, value.shape[0] // SIDE) + value.shape[1:])
    return [lax.dynamic_index_in_dim(parts, (at + step) & (SIDE - 1), 0, keepdims=False) for step in range(SIDE)]


def plane_scatter(parts, rows_count, cols_count, phase):
    total = parts[0]
    for step in range(1, SIDE):
        total = total + lax.ppermute(parts[step], BOTH, plane_shift(rows_count, cols_count, step, phase))
    return total


def plane_sum(value, rows_count, cols_count, phase):
    one, two, three = [
        lax.ppermute(value, BOTH, plane_shift(rows_count, cols_count, step, phase)) for step in range(1, SIDE)
    ]
    return (value + two) + (one + three)


def plane_gather(value, rows_count, cols_count, phase):
    return [value] + [
        lax.ppermute(value, BOTH, plane_shift(rows_count, cols_count, step, phase)) for step in range(1, SIDE)
    ]


def split(value):
    high = value.astype(jnp.bfloat16)
    return high, (value - high.astype(jnp.float32)).astype(jnp.bfloat16)


def prepare_kernel(at_ref, pattern_ref, inverse_ref, high_ref, low_ref):
    rows, cols = inverse_ref.shape

    @pl.loop(0, rows // TILE)
    def _(i):
        here = pl.ds(pl.multiple_of(i * TILE, TILE), TILE)
        for j in range(cols // TILE):
            there = slice(j * TILE, (j + 1) * TILE)
            flag = pattern_ref[at_ref[0] + i, at_ref[1] + j].astype(jnp.float32)
            high, low = split(inverse_ref[here, there] * flag)
            high_ref[here, there] = high
            low_ref[here, there] = low


def prepare(at, pattern, inverse):
    whole = pl.BlockSpec(memory_space=pltpu.VMEM)
    scalars = pl.BlockSpec(memory_space=pltpu.SMEM)
    return pl.pallas_call(
        prepare_kernel,
        in_specs=[scalars, scalars, whole],
        out_specs=[whole] * 2,
        out_shape=[jax.ShapeDtypeStruct(inverse.shape, jnp.bfloat16)] * 2,
        compiler_params=pltpu.CompilerParams(vmem_limit_bytes=VMEM_BYTES),
        cost_estimate=pl.CostEstimate(flops=4 * inverse.size, bytes_accessed=8 * inverse.size, transcendentals=0),
    )(at, pattern, inverse)


def product_kernel(at_ref, band_ref, inverse_high_ref, inverse_low_ref, *refs):
    out_refs, (high_ref, low_ref) = refs[:SIDE], refs[-2:]
    rows, cols = inverse_high_ref.shape
    part = band_ref.shape[1] // SIDE
    @pl.loop(0, SIDE * (rows // TILE))
    def _(block):
        q, i = block // (rows // TILE), block % (rows // TILE)
        to = pl.ds(pl.multiple_of((q + SIDE - at_ref[2]) % SIDE * part, part), part)
        here = pl.ds(pl.multiple_of(i * TILE, TILE), TILE)
        high, low = split(-band_ref[here, pl.ds(pl.multiple_of(q * part, part), part)].T)
        high_ref[to, here] = high
        low_ref[to, here] = low

    @pl.loop(0, cols // TILE)
    def _(j):
        there = pl.ds(pl.multiple_of(j * TILE, TILE), TILE)
        high = inverse_high_ref[:, there]
        total = jnp.dot(low_ref[...], high, preferred_element_type=jnp.float32)
        total += jnp.dot(high_ref[...], inverse_low_ref[:, there], preferred_element_type=jnp.float32)
        total += jnp.dot(high_ref[...], high, preferred_element_type=jnp.float32)
        for q in range(SIDE):
            out_refs[q][:, there] = total[q * part : (q + 1) * part]


def product(at, band, high, low):
    rows, width = band.shape
    cols = high.shape[1]
    whole = pl.BlockSpec(memory_space=pltpu.VMEM)
    return pl.pallas_call(
        product_kernel,
        in_specs=[pl.BlockSpec(memory_space=pltpu.SMEM), whole, whole, whole],
        out_specs=[whole] * SIDE,
        out_shape=[jax.ShapeDtypeStruct((width // SIDE, cols), jnp.float32)] * SIDE,
        scratch_shapes=[pltpu.VMEM((width, rows), jnp.bfloat16)] * 2,
        compiler_params=pltpu.CompilerParams(vmem_limit_bytes=VMEM_BYTES),
        cost_estimate=pl.CostEstimate(
            flops=6 * rows * width * cols, bytes_accessed=4 * (rows * width + rows * cols + width * cols), transcendentals=0
        ),
    )(at, band, high, low)


def unfold_kernel(at_ref, *refs):
    parts, (own_block_ref, other_block_ref, diag_ref, panel_ref, own_ref, other_ref) = refs[:-6], refs[-6:]
    sides, chips, kept, _ = own_ref.shape
    for step in range(sides):
        own_ref[(at_ref[1] + sides - step) % sides] = parts[step][...]
        other_ref[(at_ref[2] + sides - step) % sides] = parts[sides][step]
    blocks = diag_ref.shape[0] // LANES
    steps = blocks // 2 + 1
    rows = kept // steps
    part = own_block_ref.shape[1] // 2
    piece = panel_ref.shape[0]
    even = at_ref[0] == 0

    def both(own, other):
        return [jnp.where(even, own, other), jnp.where(even, other, own)]

    @pl.loop(0, blocks)
    def _(block):
        at = block // (blocks // 2)
        chip = block % (blocks // 2) * (LANES // (2 * part))
        here = pl.ds(pl.multiple_of(block * LANES, LANES), LANES)
        for step in range(steps):
            strips = []
            for z in range(LANES // (2 * part)):
                sources = []
                for ref in (own_ref, other_ref):
                    quarters = [
                        ref[at * (sides // 2) + q, chip + z, step * rows : (step + 1) * rows, :]
                        for q in range(sides // 2)
                    ]
                    sources.append(jnp.concatenate(quarters, axis=0))
                strips += both(*sources)
            value = jnp.concatenate(strips, axis=0)
            there = pl.ds(pl.multiple_of((block + step) % blocks * LANES, LANES), LANES)
            diag_ref[here, there] = value
            if 0 < step < blocks // 2:
                diag_ref[there, here] = value.T
        half = pl.ds(pl.multiple_of(at * part, part), part)
        strips = []
        for z in range(LANES // (2 * part)):
            strips += both(*[ref[chip + z, half, :] for ref in (own_block_ref, other_block_ref)])
        turned = jnp.concatenate(strips, axis=0).T
        panel_ref[:, here] = jnp.where(even, turned[:piece], turned[piece:])


def unfold(at, own, other, own_block, other_block, rows, width):
    whole = pl.BlockSpec(memory_space=pltpu.VMEM)
    held = pltpu.VMEM((SIDE,) + own[0].shape, jnp.float32)
    return pl.pallas_call(
        unfold_kernel,
        in_specs=[pl.BlockSpec(memory_space=pltpu.SMEM)] + [whole] * (SIDE + 3),
        out_specs=[whole, whole],
        out_shape=[
            jax.ShapeDtypeStruct((width, width), jnp.float32),
            jax.ShapeDtypeStruct((rows, width), jnp.float32),
        ],
        scratch_shapes=[held, held],
        compiler_params=pltpu.CompilerParams(vmem_limit_bytes=VMEM_BYTES),
        cost_estimate=pl.CostEstimate(
            flops=0, bytes_accessed=16 * SIDE * own[0].size + 4 * width * width, transcendentals=0
        ),
    )(at, *own, other, own_block, other_block)


def shards(ancestor_inverse, panel, diag_inverse, inverse_pattern, panel_pattern):
    rows_count = lax.axis_size("row")
    cols_count = lax.axis_size("col")
    chips = cols_count // 2
    row_at = lax.axis_index("row")
    col_at = lax.axis_index("col")
    core_at = col_at & 1
    first = core_at == 0
    y_at, x_at = row_at >> 2, row_at & (SIDE - 1)
    phase_at = (
        (jnp.where(first, x_at, y_at) - (col_at >> 2)) & (SIDE - 1),
        (jnp.where(first, y_at, x_at) - col_at) & (SIDE - 1),
    )
    block_rows, block_cols = ancestor_inverse.shape
    piece_rows, width = panel.shape
    half = width // 2
    slice_rows = half // rows_count
    inv_factor = jnp.tril(diag_inverse) + jnp.eye(width, dtype=jnp.float32)

    tile_at = jnp.stack([row_at * (block_rows // TILE), col_at * (block_cols // TILE), phase_at[0]])
    with jax.named_scope("prepare_inverse"):
        prepared = prepare(tile_at, inverse_pattern, ancestor_inverse)
    with jax.named_scope("local_scaled"):
        first_row = (row_at * cols_count + col_at) * piece_rows
        flags = lax.dynamic_slice(panel_pattern, (first_row >> 8, 0), (1, width // TILE))
        masked = panel * jnp.repeat(flags.astype(jnp.float32), TILE, axis=1)
        scaled = jnp.dot(masked, inv_factor, precision=HIGH)
    with jax.named_scope("gather_scaled"):
        left, right = scaled[:, :half], scaled[:, half:]
        mine = jnp.where(first, left, right)
        came = core_swap(jnp.where(first, right, left), cols_count)
        band_own, prepared = z_ring(by_core(first, mine, came, 0), cols_count, prepared)
        band_own = band_own.reshape(block_rows, half)
        band_other = core_swap(band_own, cols_count)
    turn = []
    for r in range(rows_count):
        for c in range(cols_count):
            y, x = divmod(r, SIDE)
            at = (x, y) if c % 2 == 0 else (y, x)
            slot = (at[0] - c // SIDE) % SIDE * SIDE + (at[1] - c % SIDE) % SIDE
            turn.append((r * cols_count + c, c * cols_count + slot))

    def sigma_slice(band):
        with jax.named_scope("product"):
            parts = product(tile_at, band, *prepared)
        with jax.named_scope("sum_row"):
            part = plane_scatter(parts, rows_count, cols_count, 0)
            part = plane_scatter(plane_parts(part, phase_at[1]), rows_count, cols_count, 1)
        with jax.named_scope("turn"):
            return lax.ppermute(part, BOTH, turn)

    own = sigma_slice(band_own)
    other = sigma_slice(band_other)
    sigma_t = by_core((row_at & 1) == 0, own, other, 0)
    with jax.named_scope("quad"):
        quad = jnp.dot(sigma_t, jnp.concatenate([band_own, band_other], axis=1), precision=HIGH)
        quad = by_core(first, quad[:, :half], quad[:, half:], 1)
        share = width // rows_count
        factor_rows = lax.dynamic_slice(diag_inverse, (row_at * share, 0), (share, width))
        below = row_at * share + lax.broadcasted_iota(jnp.int32, (share, width), 0)
        below = below - lax.broadcasted_iota(jnp.int32, (share, width), 1)
        factor_rows = jnp.where(below >= 0, factor_rows, 0.0) + (below == 0).astype(jnp.float32)
        factor_tile = jnp.concatenate(
            [
                lax.dynamic_slice(factor_rows, (0, part * half + col_at * slice_rows), (share, slice_rows))
                for part in range(2)
            ],
            axis=1,
        )
        base = lax.dot_general(factor_tile, factor_rows, (((0,), (0,)), ((), ())), precision=HIGH)
        term = base - quad
    with jax.named_scope("keep_half"):
        kept = width // 2 + LANES
        wrapped = jnp.concatenate([term, term[:, : width // 2]], axis=1)
        starts = [(part * half + col_at * slice_rows) & -LANES for part in range(2)]
        term = jnp.concatenate(
            [
                lax.dynamic_slice(wrapped, (part * slice_rows, starts[part]), (slice_rows, kept))
                for part in range(2)
            ],
            axis=0,
        )
    with jax.named_scope("sum_diag"):
        axis_at = jnp.where(first, x_at, y_at)
        term = plane_scatter(plane_parts(term, axis_at), rows_count, cols_count, 0)
        term = plane_sum(term, rows_count, cols_count, 1)
        term = term.reshape(-1, kept // LANES, LANES).transpose(1, 0, 2).reshape(-1, LANES)
    with jax.named_scope("gather_diag"):
        held = z_ring_deliver(term, sigma_t, cols_count)
        block = held[:, : 2 * slice_rows]
        other_block = core_swap(block, cols_count)
        parts = plane_gather(held[:, 2 * slice_rows :], rows_count, cols_count, 0)
        other_parts = core_swap(jnp.stack(parts), cols_count)
        places = jnp.stack([core_at, axis_at, jnp.where(first, y_at, x_at)])
        sigma_diag, sigma_panel = unfold(places, parts, other_parts, block, other_block, piece_rows, width)
    return sigma_panel, sigma_diag


def solution(mesh):
    return jax.shard_map(
        shards,
        mesh=mesh,
        in_specs=(P("row", "col"), P(("row", "col"), None), P(), P(), P()),
        out_specs=(P(("row", "col"), None), P()),
        check_vma=False,
    )
```
